32 devices in a mesh: dp: 4 (over y, x), expert: 8 (over z, core).
Axes of the slice: x: 2, y: 2, z: 4, core: 2. Of those that a mesh axis runs over, the one named last changes fastest.
Arguments:
- tokens: bfloat16 [4096, 2048], P(('dp', 'expert')), may hold values from -6 to 6
- expert_ids: int32 [4096, 2], P(('dp', 'expert')), may hold values from 0 to 7, all different within a row; in each aligned block of 128 rows (0 to 127, 128 to 255, ...) at most 48 rows name the same one
- gates: bfloat16 [4096, 2], P(('dp', 'expert')), may hold values from 0.049804688 to 1
- cotangent: bfloat16 [4096, 2048], P(('dp', 'expert')), may hold values from -6 to 6
- w_gate: bfloat16 [8, 2048, 768], P('expert'), may hold values from -0.125 to 0.125
- w_up: bfloat16 [8, 2048, 768], P('expert'), may hold values from -0.125 to 0.125
- w_down: bfloat16 [8, 768, 2048], P('expert'), may hold values from -0.21875 to 0.21875
Outputs:
- grad_tokens: bfloat16 [4096, 2048], P(('dp', 'expert'))
- grad_gates: bfloat16 [4096, 2], P(('dp', 'expert'))
- grad_w_gate: bfloat16 [8, 2048, 768], P('expert', 'dp')
- grad_w_up: bfloat16 [8, 2048, 768], P('expert', 'dp')
- grad_w_down: bfloat16 [8, 768, 2048], P('expert', None, 'dp')
The draws below stay inside these ranges and needn't reach their ends.
Inputs may be any that keep to these rules, and one draw needn't show every extreme that they name: `expert_ids`: within the 128 rows of one device no expert is named by more than 48 rows, and in some of these aligned blocks an expert is named by exactly 48 rows.
All inputs are finite; a program needn't handle non-finite values.
Results may differ from the reference program's by a relative error of at most 0.013.
Values may be sent and summed in bfloat16 or wider, within the bound.
A program may use at most 128 MiB of HBM per device.

```python
import math
import jax
import jax.numpy as jnp
import numpy as np
from jax import lax

D = 2048
FF = 768
TOK_DEV = 128
TOP = 2
EXPERTS = 8
CAP = 48
TOKENS = 4096
N_DP = 4
N_EXPERT = 8


def block_levels(key, shape, cuts, smallest, top_value):
    loudness = 1.0
    for axis_at, shards_of in cuts:
        draws = jax.random.uniform(jax.random.fold_in(jax.random.fold_in(key, 6), axis_at), (shards_of,), jnp.float32, smallest / len(cuts), top_value / len(cuts))
        loudness = loudness * jnp.repeat(jnp.exp(draws), shape[axis_at] // shards_of).reshape((-1,) + (1,) * (len(shape) - 1 - axis_at))
    return loudness


def shared_out(stream_key, own, number, rows, number_of, top, reach, slope):
    order = jax.random.permutation(stream_key, number_of)
    heavy_load, common = load_shares(number_of, rows * top, reach, slope, True), load_shares(number_of, rows * top, reach, slope, False)
    places = jnp.arange(number_of)

    def named(lengths, offset_by):
        used = int((lengths > 0).sum())
        fixed = max(1, used // 4)
        moved = fixed + (places - fixed + offset_by * (used - fixed)) % max(1, number_of - fixed)
        return jnp.zeros((number_of,), jnp.int32).at[order[jnp.where(places < fixed, places, moved)]].set(jnp.asarray(lengths, jnp.int32))

    lengths = jnp.where(number % 4 == 0, named(heavy_load, number // 4), named(common, number - number // 4 - 1))
    mixed = jax.random.permutation(jax.random.fold_in(own, 3), number_of)
    giver, receiver = mixed[0:number_of // 2 * 2:2], mixed[1:number_of // 2 * 2:2]
    room = jnp.minimum(lengths[giver] - 1, reach - lengths[receiver]) // 2
    room = jnp.where((giver == order[0]) | (receiver == order[0]) | (lengths[receiver] == 0), 0, jnp.maximum(room, 0))
    moved = jax.random.randint(jax.random.fold_in(own, 4), (number_of // 2,), 0, 1 << 20) % (room + 1)
    lengths = lengths.at[giver].add(-moved).at[receiver].add(moved)
    labels = jnp.searchsorted(jnp.cumsum(lengths), jnp.arange(rows * top), side="right").astype(jnp.int32)
    table = labels.reshape(top, rows).T
    table = table[jax.random.permutation(jax.random.fold_in(own, 1), rows)]
    offset_by = jax.random.randint(jax.random.fold_in(own, 2), (rows, 1), 0, top)
    return jnp.take_along_axis(table, (jnp.arange(top)[None, :] + offset_by) % top, axis=1)


def load_shares(count, total, limit, skew, full):
    portions = [(1 << 20) // math.isqrt(grade ** skew) + 1 for grade in range(1, count + 1)]
    largest = limit if full else min(limit, max(-(-total // count), total * portions[0] // sum(portions)))
    least = 1 if total - largest >= count - 1 else 0
    counts, rest = [largest] + [least] * (count - 1), total - largest - least * (count - 1)
    while rest > 0:
        free = [i for i in range(1, count) if counts[i] < largest] or [i for i in range(1, count) if counts[i] < limit]
        mass, remaining = sum([portions[i] for i in free]), rest
        for i in free:
            more = min(limit - counts[i], max(1, remaining * portions[i] // mass), rest)
            counts[i] = counts[i] + more
            rest = rest - more
    return np.array(counts)


def scatter_about(own_key, shape, spread, limit, shards=(), held_as=jnp.bfloat16):
    entries = spread * jax.random.normal(own_key, shape, jnp.float32)
    if shards:
        entries = entries * block_levels(own_key, shape, shards, -0.22, 0.18)
    return jnp.clip(entries, -limit, limit).astype(held_as)


def setup_inputs(seed: int = 0) -> dict:
    streams_of = jax.random.split(jax.random.key(seed), 8)
    tokens = scatter_about(streams_of[0], (TOKENS, D), 1.0, 6.0, ((0, 32),))
    expert_ids_keys = jax.random.split(jax.random.fold_in(streams_of[1], 1), TOKENS // TOK_DEV)
    expert_ids_turns = jax.random.permutation(jax.random.fold_in(streams_of[1], 3), TOKENS // TOK_DEV)
    expert_ids = jax.vmap(lambda own, number: shared_out(jax.random.fold_in(streams_of[1], 2), own, number, TOK_DEV, EXPERTS, TOP, CAP, 2))(expert_ids_keys, expert_ids_turns).reshape((TOKENS, TOP))
    gates = jnp.clip(jnp.exp(math.log(1.0) - 2.9996462 * jax.random.uniform(streams_of[2], (TOKENS, TOP), jnp.float32) ** block_levels(streams_of[2], (TOKENS, TOP), ((0, 32),), -0.2, 0.2)), 0.049804688, 1.0).astype(jnp.bfloat16)
    cotangent = scatter_about(streams_of[3], (TOKENS, D), 1.0, 6.0, ((0, 32),))
    w_gate = scatter_about(streams_of[4], (EXPERTS, D, FF), D ** -0.5, 0.125, ((0, 8),))
    w_up = scatter_about(streams_of[5], (EXPERTS, D, FF), D ** -0.5, 0.125, ((0, 8),))
    w_down = scatter_about(streams_of[6], (EXPERTS, FF, D), FF ** -0.5, 0.21875, ((0, 8),))
    return {"tokens": tokens, "expert_ids": expert_ids, "gates": gates, "cotangent": cotangent, "w_gate": w_gate, "w_up": w_up, "w_down": w_down}


def contract_rows(left, right):
    return lax.dot_general(left, right, (((0,), (0,)), ((), ())), preferred_element_type=jnp.float32)


def expert_pass(rows, cot_rows, gate_column, gate_mat, up_mat, down_mat):
    pre_gate = jnp.dot(rows, gate_mat, preferred_element_type=jnp.float32)
    pre_up = jnp.dot(rows, up_mat, preferred_element_type=jnp.float32)
    sigmoid_gate = jax.nn.sigmoid(pre_gate)
    activated = pre_gate * sigmoid_gate
    hidden = (activated * pre_up).astype(jnp.bfloat16)
    expert_out = jnp.dot(hidden, down_mat, preferred_element_type=jnp.float32)
    cot_float = cot_rows.astype(jnp.float32)
    score_grad = jnp.sum(expert_out * cot_float, axis=1)
    scaled = (gate_column.astype(jnp.float32)[:, None] * cot_float).astype(jnp.bfloat16)
    grad_hidden = jnp.dot(scaled, down_mat.T, preferred_element_type=jnp.float32)
    grad_pre_gate = (grad_hidden * pre_up * sigmoid_gate * (1.0 + pre_gate * (1.0 - sigmoid_gate))).astype(jnp.bfloat16)
    grad_pre_up = (grad_hidden * activated).astype(jnp.bfloat16)
    row_grad = (jnp.dot(grad_pre_gate, gate_mat.T, preferred_element_type=jnp.float32)
                + jnp.dot(grad_pre_up, up_mat.T, preferred_element_type=jnp.float32)).astype(jnp.bfloat16)
    return hidden, scaled, grad_pre_gate, grad_pre_up, row_grad, score_grad


def reference(tokens, expert_ids, gates, cotangent, w_gate, w_up, w_down):
    blocks = N_DP * N_EXPERT
    pair_count = TOK_DEV * TOP
    block_ids = expert_ids.reshape(blocks, pair_count)
    picked = (block_ids[:, :, None] == jnp.arange(EXPERTS, dtype=jnp.int32)[None, None, :]).astype(jnp.int32)
    before = jnp.cumsum(picked, axis=1) - picked
    position = jnp.sum(before * picked, axis=2).astype(jnp.int32)
    target = (block_ids * CAP + position).astype(jnp.int32)
    pair_global = jnp.arange(blocks * pair_count, dtype=jnp.int32).reshape(blocks, pair_count)
    block_index = jnp.arange(blocks, dtype=jnp.int32)[:, None]
    table = jnp.full((blocks, EXPERTS * CAP), -1, jnp.int32).at[block_index, target].set(pair_global)
    table = table.reshape(blocks, EXPERTS, CAP).transpose(1, 0, 2).reshape(EXPERTS, blocks * CAP)
    flat_gates = gates.reshape(-1)
    group_rows = N_EXPERT * CAP

    def group_total(left, right):
        total = jnp.zeros((left.shape[1], right.shape[1]), jnp.float32)
        for group in range(N_DP):
            part = contract_rows(left[group * group_rows:(group + 1) * group_rows],
                                 right[group * group_rows:(group + 1) * group_rows]).astype(jnp.bfloat16)
            total = total + lax.optimization_barrier(part).astype(jnp.float32)
        return total.astype(jnp.bfloat16)

    def one_expert(carry, inputs):
        grad_rows, score_acc = carry
        pair_index, gate_mat, up_mat, down_mat = inputs
        valid = pair_index >= 0
        safe_pair = jnp.where(valid, pair_index, 0).astype(jnp.int32)
        token_index = (safe_pair // TOP).astype(jnp.int32)
        rows = jnp.where(valid[:, None], tokens[token_index], jnp.zeros((), jnp.bfloat16))
        cot_rows = jnp.where(valid[:, None], cotangent[token_index], jnp.zeros((), jnp.bfloat16))
        gate_column = jnp.where(valid, flat_gates[safe_pair], jnp.zeros((), jnp.bfloat16))
        hidden, scaled, grad_pre_gate, grad_pre_up, row_grad, score_grad = expert_pass(
            rows, cot_rows, gate_column, gate_mat, up_mat, down_mat)
        grad_rows = grad_rows.at[token_index].add(jnp.where(valid[:, None], row_grad.astype(jnp.float32), jnp.zeros((), jnp.float32)))
        score_acc = score_acc.at[safe_pair].add(jnp.where(valid, score_grad, jnp.zeros((), jnp.float32)))
        grads = (group_total(rows, grad_pre_gate), group_total(rows, grad_pre_up), group_total(hidden, scaled))
        return (grad_rows, score_acc), grads

    start = (jnp.zeros((TOKENS, D), jnp.float32), jnp.zeros((TOKENS * TOP,), jnp.float32))
    (grad_rows, score_acc), (grad_w_gate, grad_w_up, grad_w_down) = lax.scan(
        one_expert, start, (table, w_gate, w_up, w_down))
    return (grad_rows.astype(jnp.bfloat16), score_acc.reshape(TOKENS, TOP).astype(jnp.bfloat16),
            grad_w_gate, grad_w_up, grad_w_down)
```

```python
import functools

import jax
import jax.numpy as jnp
from jax import lax
from jax.experimental import pallas as pl
from jax.experimental.pallas import tpu as pltpu
from jax.sharding import PartitionSpec as P

MESH = pl.DeviceIdType.MESH
F32 = jnp.float32
BF16 = jnp.bfloat16


def tile_of(size, most):
    step = min(size, most)
    while size % step:
        step -= 128
    return step


def dot_nt(left, right):
    return lax.dot_general(left, right, (((1,), (1,)), ((), ())), preferred_element_type=F32)


def dot_tn(left, right):
    return lax.dot_general(left, right, (((0,), (0,)), ((), ())), preferred_element_type=F32)


def layer_kernel(
    owners, groups, capacity,
    ids_ref, gates_ref, tok_ref, cot_ref, wg_hbm, wu_hbm, wd_hbm,
    gtok_ref, ggate_ref, gwg_ref, gwu_ref, gwd_ref,
    wg, wu, wd, w_sem,
    pick, gate_col, send_tok, send_cot, rows, scaled, pre_gate, pre_up, score,
    x_rows, x_scaled, x_hid, x_gg, x_gu, own_sem,
    back_send, back_recv, score_send, score_recv, acc_gate, acc_up,
    tok_s, tok_r, cot_s, cot_r, back_s, back_r, sc_s, sc_r,
    fr_s, fr_r, fc_s, fc_r, h_s, h_r, gg_s, gg_r, gu_s, gu_r,
):
    me = lax.axis_index("expert")
    grp = lax.axis_index("dp")
    tok_count, width = tok_ref.shape
    slots = owners * capacity
    hid_width = wg.shape[1]
    part = width // groups
    hid_tile = tile_of(hid_width, 256)
    wide_tile = tile_of(width, 512)

    weight_copies = [
        pltpu.make_async_copy(src.at[0], dst, w_sem.at[i])
        for i, (src, dst) in enumerate(((wg_hbm, wg), (wu_hbm, wu), (wd_hbm, wd)))
    ]
    for copy in weight_copies:
        copy.start()

    barrier = pltpu.get_barrier_semaphore()
    for k in range(1, owners):
        pl.semaphore_signal(
            barrier, inc=1, device_id={"expert": lax.rem(me + k, owners)}, device_id_type=MESH
        )
    for j in range(1, groups):
        pl.semaphore_signal(
            barrier, inc=1, device_id={"dp": lax.rem(grp + j, groups)}, device_id_type=MESH
        )

    expert_no = lax.broadcasted_iota(jnp.int32, (owners, tok_count), 0)
    first = ids_ref[0:1, :] == expert_no
    second = ids_ref[1:2, :] == expert_no
    named = jnp.where(first, 1.0, 0.0) + jnp.where(second, 1.0, 0.0)
    gate_of = jnp.where(first, gates_ref[0:1, :], 0.0) + jnp.where(second, gates_ref[1:2, :], 0.0)
    earlier = jnp.where(
        lax.broadcasted_iota(jnp.int32, (tok_count, tok_count), 0)
        < lax.broadcasted_iota(jnp.int32, (tok_count, tok_count), 1),
        1.0, 0.0,
    ).astype(BF16)
    position = jnp.dot(named.astype(BF16), earlier, preferred_element_type=F32)
    position = jnp.where(named > 0.5, position, -1.0)
    slot_no = lax.broadcasted_iota(jnp.int32, (capacity, tok_count), 0).astype(F32)
    for e in range(owners):
        chosen = jnp.where(slot_no == position[e:e + 1, :], 1.0, 0.0)
        pick[e * capacity:(e + 1) * capacity, :] = chosen.astype(BF16)
        gate_col[e * capacity:(e + 1) * capacity, :] = jnp.broadcast_to(
            jnp.sum(chosen * gate_of[e:e + 1, :], axis=1, keepdims=True), (capacity, 128)
        )

    @pl.loop(0, width // wide_tile)
    def _(n):
        cols = pl.ds(pl.multiple_of(n * wide_tile, wide_tile), wide_tile)
        picked = jnp.dot(pick[...], tok_ref[:, cols], preferred_element_type=F32)
        send_tok[:, :, cols] = picked.astype(BF16).reshape(owners, capacity, wide_tile)

    pl.semaphore_wait(barrier, owners - 1 + groups - 1)

    def across(src, dst, send, recv, k):
        return pltpu.make_async_remote_copy(
            src_ref=src, dst_ref=dst, send_sem=send, recv_sem=recv,
            device_id={"expert": lax.rem(me + k, owners)}, device_id_type=MESH,
        )

    def aside(src, dst, send, recv, j):
        return pltpu.make_async_remote_copy(
            src_ref=src, dst_ref=dst, send_sem=send, recv_sem=recv,
            device_id={"dp": lax.rem(grp + j, groups)}, device_id_type=MESH,
        )

    def send_block(sent, held, send, recv, k):
        return across(sent.at[lax.rem(me + k, owners)], held.at[me], send.at[k], recv.at[k], k)

    def take_block(sent, held, send, recv, k):
        source = lax.rem(me + owners - k, owners)
        across(sent.at[source], held.at[source], send.at[k], recv.at[k], k).wait_recv()
        return source

    def share(held, parts, send, recv, k, j):
        source = lax.rem(me + owners - k, owners)
        target = lax.rem(grp + j, groups)
        cols = pl.ds(pl.multiple_of(target * part, part), part)
        return aside(
            held.at[source, :, cols], parts.at[grp, source], send.at[k, j], recv.at[k, j], j
        )

    def take_share(held, parts, send, recv, k, j):
        source = lax.rem(me + owners - k, owners)
        origin = lax.rem(grp + groups - j, groups)
        aside(
            held.at[source, :, pl.ds(0, part)], parts.at[origin, source],
            send.at[k, j], recv.at[k, j], j,
        ).wait_recv()

    def spread(held, send, recv, j):
        return aside(held.at[grp], held.at[grp], send.at[j], recv.at[j], j)

    def take_spread(held, send, recv, j):
        origin = lax.rem(grp + groups - j, groups)
        aside(held.at[origin], held.at[origin], send.at[j], recv.at[j], j).wait_recv()
        return origin

    for k in range(1, owners):
        send_block(send_tok, rows, tok_s, tok_r, k).start()

    @pl.loop(0, width // wide_tile)
    def _(n):
        cols = pl.ds(pl.multiple_of(n * wide_tile, wide_tile), wide_tile)
        picked = jnp.dot(pick[...], cot_ref[:, cols], preferred_element_type=F32)
        picked = picked * gate_col[:, 0:1]
        send_cot[:, :, cols] = picked.astype(BF16).reshape(owners, capacity, wide_tile)

    rows[me] = send_tok[me]
    scaled[me] = send_cot[me]
    for j in range(1, groups):
        share(rows, x_rows, fr_s, fr_r, 0, j).start()
    for k in range(1, owners):
        take_block(send_tok, rows, tok_s, tok_r, k)
        for j in range(1, groups):
            share(rows, x_rows, fr_s, fr_r, k, j).start()
        send_block(send_tok, rows, tok_s, tok_r, k).wait_send()
        send_block(send_cot, scaled, cot_s, cot_r, k).start()

    mine = pl.ds(pl.multiple_of(grp * part, part), part)
    own_rows = pltpu.make_async_copy(rows.at[:, :, mine], x_rows.at[grp], own_sem.at[0])
    own_rows.start()
    weight_copies[0].wait()
    weight_copies[1].wait()

    @pl.loop(0, hid_width // hid_tile)
    def _(n):
        cols = pl.ds(pl.multiple_of(n * hid_tile, hid_tile), hid_tile)
        held = rows[...].reshape(slots, width)
        gate = jnp.dot(held, wg[:, cols], preferred_element_type=F32)
        up = jnp.dot(held, wu[:, cols], preferred_element_type=F32)
        pre_gate[:, cols] = gate
        pre_up[:, cols] = up
        x_hid[grp, :, cols] = (gate * jax.nn.sigmoid(gate) * up).astype(BF16)

    for j in range(1, groups):
        spread(x_hid, h_s, h_r, j).start()
    for j in range(1, groups):
        share(scaled, x_scaled, fc_s, fc_r, 0, j).start()
    for k in range(1, owners):
        take_block(send_cot, scaled, cot_s, cot_r, k)
        for j in range(1, groups):
            share(scaled, x_scaled, fc_s, fc_r, k, j).start()
    own_scaled = pltpu.make_async_copy(scaled.at[:, :, mine], x_scaled.at[grp], own_sem.at[1])
    own_scaled.start()
    weight_copies[2].wait()
    score[...] = jnp.zeros_like(score)

    @pl.loop(0, hid_width // hid_tile)
    def _(n):
        cols = pl.ds(pl.multiple_of(n * hid_tile, hid_tile), hid_tile)
        grad_hidden = dot_nt(scaled[...].reshape(slots, width), wd[cols, :])
        gate = pre_gate[:, cols]
        sig = jax.nn.sigmoid(gate)
        x_gg[grp, :, cols] = (
            grad_hidden * pre_up[:, cols] * sig * (1.0 + gate * (1.0 - sig))
        ).astype(BF16)
        x_gu[grp, :, cols] = (grad_hidden * (gate * sig)).astype(BF16)
        score[...] += jnp.broadcast_to(
            jnp.sum(x_hid[grp, :, cols].astype(F32) * grad_hidden, axis=1, keepdims=True),
            (slots, 128),
        )

    for j in range(1, groups):
        spread(x_gg, gg_s, gg_r, j).start()
        spread(x_gu, gu_s, gu_r, j).start()

    @pl.loop(0, width // wide_tile)
    def _(n):
        cols = pl.ds(pl.multiple_of(n * wide_tile, wide_tile), wide_tile)
        grad = dot_nt(x_gg[grp], wg[cols, :]) + dot_nt(x_gu[grp], wu[cols, :])
        back_send[:, :, cols] = grad.astype(BF16).reshape(owners, capacity, wide_tile)

    on_diagonal = lax.broadcasted_iota(jnp.int32, (capacity, 128), 0) == lax.broadcasted_iota(
        jnp.int32, (capacity, 128), 1
    )
    for e in range(owners):
        line = jnp.sum(
            jnp.where(on_diagonal, score[e * capacity:(e + 1) * capacity, :], 0.0),
            axis=0, keepdims=True,
        )
        score_send[e] = jnp.broadcast_to(line, (8, 128))
    for k in range(1, owners):
        send_block(back_send, back_recv, back_s, back_r, k).start()
        send_block(score_send, score_recv, sc_s, sc_r, k).start()
    back_recv[me] = back_send[me]
    score_recv[me] = score_send[me]

    own_rows.wait()
    own_scaled.wait()
    for j in range(1, groups):
        take_spread(x_hid, h_s, h_r, j)
        for k in range(owners):
            take_share(rows, x_rows, fr_s, fr_r, k, j)
            take_share(scaled, x_scaled, fc_s, fc_r, k, j)

    @pl.loop(0, hid_width // hid_tile)
    def _(n):
        cols = pl.ds(pl.multiple_of(n * hid_tile, hid_tile), hid_tile)
        gwd_ref[cols, :] = dot_tn(
            x_hid[:, :, cols].reshape(groups * slots, hid_tile),
            x_scaled[...].reshape(groups * slots, part),
        ).astype(BF16)

    def add_group(origin, begin, end):
        @pl.loop(0, hid_width // hid_tile)
        def _(n):
            cols = pl.ds(pl.multiple_of(n * hid_tile, hid_tile), hid_tile)
            left = x_rows[origin].reshape(slots, part)
            gate = dot_tn(left, x_gg[origin, :, cols])
            up = dot_tn(left, x_gu[origin, :, cols])
            if not begin:
                gate = gate + acc_gate[:, cols]
                up = up + acc_up[:, cols]
            if end:
                gwg_ref[:, cols] = gate.astype(BF16)
                gwu_ref[:, cols] = up.astype(BF16)
            else:
                acc_gate[:, cols] = gate
                acc_up[:, cols] = up

    add_group(grp, True, groups == 1)

    for k in range(1, owners):
        take_block(back_send, back_recv, back_s, back_r, k)
        take_block(score_send, score_recv, sc_s, sc_r, k)

    @pl.loop(0, width // wide_tile)
    def _(n):
        cols = pl.ds(pl.multiple_of(n * wide_tile, wide_tile), wide_tile)
        gtok_ref[:, cols] = dot_tn(
            pick[...], back_recv[:, :, cols].reshape(slots, wide_tile)
        ).astype(BF16)

    first_sum = jnp.zeros((1, tok_count), F32)
    second_sum = jnp.zeros((1, tok_count), F32)
    for e in range(owners):
        column = jnp.sum(
            jnp.where(on_diagonal, jnp.broadcast_to(score_recv[e, 0:1, :], (capacity, 128)), 0.0),
            axis=1, keepdims=True,
        )
        by_token = jnp.sum(
            pick[e * capacity:(e + 1) * capacity, :].astype(F32) * column, axis=0, keepdims=True
        )
        first_sum = first_sum + jnp.where(ids_ref[0:1, :] == e, by_token, 0.0)
        second_sum = second_sum + jnp.where(ids_ref[1:2, :] == e, by_token, 0.0)
    ggate_ref[0:1, :] = first_sum / gates_ref[0:1, :]
    ggate_ref[1:2, :] = second_sum / gates_ref[1:2, :]

    for j in range(1, groups):
        origin = take_spread(x_gg, gg_s, gg_r, j)
        take_spread(x_gu, gu_s, gu_r, j)
        add_group(origin, False, j == groups - 1)

    for k in range(1, owners):
        send_block(send_cot, scaled, cot_s, cot_r, k).wait_send()
        send_block(back_send, back_recv, back_s, back_r, k).wait_send()
        send_block(score_send, score_recv, sc_s, sc_r, k).wait_send()
    for j in range(1, groups):
        spread(x_hid, h_s, h_r, j).wait_send()
        spread(x_gg, gg_s, gg_r, j).wait_send()
        spread(x_gu, gu_s, gu_r, j).wait_send()
        for k in range(owners):
            share(rows, x_rows, fr_s, fr_r, k, j).wait_send()
            share(scaled, x_scaled, fc_s, fc_r, k, j).wait_send()


def kernel_body(tokens, expert_ids, gates, cotangent, w_gate, w_up, w_down):
    tok_rows, width = tokens.shape
    owners = lax.axis_size("expert")
    groups = lax.axis_size("dp")
    capacity = slots_of(tok_rows, expert_ids.shape[1], owners)
    hid_width = w_gate.shape[2]
    part = width // groups
    slots = owners * capacity
    vmem = pl.BlockSpec(memory_space=pltpu.VMEM)
    dma = pltpu.SemaphoreType.DMA
    blocks = pltpu.VMEM((owners, capacity, width), BF16)
    parts = pltpu.VMEM((groups, owners, capacity, part), BF16)
    hids = pltpu.VMEM((groups, slots, hid_width), BF16)
    lines = pltpu.VMEM((owners, 8, 128), F32)
    per_owner, per_group, per_share = dma((owners,)), dma((groups,)), dma((owners, groups))
    grad_tokens, grad_gates, grad_gate, grad_up, grad_down = pl.pallas_call(
        functools.partial(layer_kernel, owners, groups, capacity),
        out_shape=(
            jax.ShapeDtypeStruct((tok_rows, width), BF16),
            jax.ShapeDtypeStruct((2, tok_rows), F32),
            jax.ShapeDtypeStruct((part, hid_width), BF16),
            jax.ShapeDtypeStruct((part, hid_width), BF16),
            jax.ShapeDtypeStruct((hid_width, part), BF16),
        ),
        in_specs=[vmem] * 4 + [pl.BlockSpec(memory_space=pl.ANY)] * 3,
        out_specs=(vmem,) * 5,
        scratch_shapes=[
            pltpu.VMEM((width, hid_width), BF16),
            pltpu.VMEM((width, hid_width), BF16),
            pltpu.VMEM((hid_width, width), BF16),
            dma((3,)),
            pltpu.VMEM((slots, tok_rows), BF16),
            pltpu.VMEM((slots, 128), F32),
            blocks, blocks, blocks, blocks,
            pltpu.VMEM((slots, hid_width), F32),
            pltpu.VMEM((slots, hid_width), F32),
            pltpu.VMEM((slots, 128), F32),
            parts, parts, hids, hids, hids,
            dma((2,)),
            blocks, blocks, lines, lines,
            pltpu.VMEM((part, hid_width), F32),
            pltpu.VMEM((part, hid_width), F32),
        ]
        + [per_owner] * 8 + [per_share] * 4 + [per_group] * 6,
        compiler_params=pltpu.CompilerParams(
            collective_id=0, has_side_effects=True, vmem_limit_bytes=56 * 1024 * 1024
        ),
        cost_estimate=pl.CostEstimate(
            flops=16 * slots * width * hid_width,
            bytes_accessed=6 * width * hid_width * 2,
            transcendentals=2 * slots * hid_width,
        ),
        name="expert_layer",
    )(
        expert_ids.T, gates.astype(F32).T, tokens, cotangent, w_gate, w_up, w_down
    )
    return (grad_tokens, grad_gates.T.astype(BF16), grad_gate[None], grad_up[None], grad_down[None])


def contract_rows(left, right):
    return lax.dot_general(
        left, right, (((0,), (0,)), ((), ())), preferred_element_type=jnp.float32
    )


def expert_pass(rows, cot_rows, gate_column, gate_mat, up_mat, down_mat):
    pre_gate = jnp.dot(rows, gate_mat, preferred_element_type=jnp.float32)
    pre_up = jnp.dot(rows, up_mat, preferred_element_type=jnp.float32)
    sigmoid_gate = jax.nn.sigmoid(pre_gate)
    activated = pre_gate * sigmoid_gate
    hidden = (activated * pre_up).astype(jnp.bfloat16)
    expert_out = jnp.dot(hidden, down_mat, preferred_element_type=jnp.float32)
    cot_float = cot_rows.astype(jnp.float32)
    score_grad = jnp.sum(expert_out * cot_float, axis=1)
    scaled = (gate_column.astype(jnp.float32)[:, None] * cot_float).astype(jnp.bfloat16)
    grad_hidden = jnp.dot(scaled, down_mat.T, preferred_element_type=jnp.float32)
    grad_pre_gate = (
        grad_hidden * pre_up * sigmoid_gate * (1.0 + pre_gate * (1.0 - sigmoid_gate))
    ).astype(jnp.bfloat16)
    grad_pre_up = (grad_hidden * activated).astype(jnp.bfloat16)
    row_grad = (
        jnp.dot(grad_pre_gate, gate_mat.T, preferred_element_type=jnp.float32)
        + jnp.dot(grad_pre_up, up_mat.T, preferred_element_type=jnp.float32)
    ).astype(jnp.bfloat16)
    return (hidden, scaled, grad_pre_gate, grad_pre_up, row_grad, score_grad)


def by_owner(values, owners, capacity):
    return values.reshape((owners, capacity) + values.shape[1:])


def sum_weights(part_gate, part_up, part_down):
    return (
        lax.psum_scatter(
            part_gate.astype(jnp.bfloat16), "dp", scatter_dimension=0, tiled=True
        ).astype(jnp.float32),
        lax.psum_scatter(
            part_up.astype(jnp.bfloat16), "dp", scatter_dimension=0, tiled=True
        ).astype(jnp.float32),
        lax.psum_scatter(
            part_down.astype(jnp.bfloat16), "dp", scatter_dimension=1, tiled=True
        ).astype(jnp.float32),
    )


def send_back(row_grad, score_grad, owners, capacity):
    score_half = score_grad.astype(jnp.bfloat16)
    back_rows = lax.all_to_all(
        by_owner(row_grad, owners, capacity), "expert", split_axis=0, concat_axis=0, tiled=True
    )
    back_scores = lax.all_to_all(
        by_owner(score_half, owners, capacity), "expert", split_axis=0, concat_axis=0, tiled=True
    )
    return (back_rows, back_scores)


def plain_body(tokens, expert_ids, gates, cotangent, w_gate, w_up, w_down):
    tok_rows, model_width = tokens.shape
    top_count = expert_ids.shape[1]
    owners = lax.axis_size("expert")
    capacity = min(tok_rows, 3 * tok_rows * top_count // (2 * owners))
    slot_count = owners * capacity
    flat_ids = expert_ids.reshape(-1)
    pair_count = flat_ids.shape[0]
    picked = (flat_ids[:, None] == jnp.arange(owners, dtype=jnp.int32)[None, :]).astype(jnp.int32)
    before = jnp.cumsum(picked, axis=0) - picked
    position = jnp.sum(before * picked, axis=1)
    target = flat_ids * capacity + position
    source_row = jnp.arange(pair_count, dtype=jnp.int32) // top_count
    send_rows = (
        jnp.zeros((slot_count, model_width), jnp.bfloat16).at[target].set(tokens[source_row])
    )
    send_cot = (
        jnp.zeros((slot_count, model_width), jnp.bfloat16).at[target].set(cotangent[source_row])
    )
    send_gate = jnp.zeros((slot_count,), jnp.bfloat16).at[target].set(gates.reshape(-1))
    recv_gate = lax.all_to_all(
        by_owner(send_gate, owners, capacity), "expert", split_axis=0, concat_axis=0, tiled=True
    )
    recv_rows = lax.all_to_all(
        by_owner(send_rows, owners, capacity), "expert", split_axis=0, concat_axis=0, tiled=True
    )
    recv_cot = lax.all_to_all(
        by_owner(send_cot, owners, capacity), "expert", split_axis=0, concat_axis=0, tiled=True
    )
    rows = recv_rows.reshape(slot_count, model_width)
    cot_rows = recv_cot.reshape(slot_count, model_width)
    gate_column = recv_gate.reshape(slot_count)
    hidden, scaled, grad_pre_gate, grad_pre_up, row_grad, score_grad = expert_pass(
        rows, cot_rows, gate_column, w_gate[0], w_up[0], w_down[0]
    )
    part_gate = contract_rows(rows, grad_pre_gate)
    part_up = contract_rows(rows, grad_pre_up)
    part_down = contract_rows(hidden, scaled)
    back_rows, back_scores = send_back(row_grad, score_grad, owners, capacity)
    summed = sum_weights(part_gate, part_up, part_down)
    pair_rows = back_rows.reshape(slot_count, model_width)[target].reshape(
        tok_rows, top_count, model_width
    )
    grad_tokens = jnp.sum(pair_rows.astype(jnp.float32), axis=1).astype(jnp.bfloat16)
    grad_gates = back_scores.reshape(slot_count)[target].reshape(tok_rows, top_count)
    grad_w_gate = summed[0].astype(jnp.bfloat16)[None]
    grad_w_up = summed[1].astype(jnp.bfloat16)[None]
    grad_w_down = summed[2].astype(jnp.bfloat16)[None]
    return (grad_tokens, grad_gates, grad_w_gate, grad_w_up, grad_w_down)


def slots_of(tok_rows, top_count, owners):
    return min(tok_rows, 3 * tok_rows * top_count // (2 * owners))


def body(tokens, expert_ids, gates, cotangent, w_gate, w_up, w_down):
    capacity = slots_of(tokens.shape[0], expert_ids.shape[1], lax.axis_size("expert"))
    chosen = kernel_body if capacity % 16 == 0 else plain_body
    return chosen(tokens, expert_ids, gates, cotangent, w_gate, w_up, w_down)


def solution(mesh):
    placed = (
        P(("dp", "expert"), None),
        P(("dp", "expert"), None),
        P(("dp", "expert"), None),
        P(("dp", "expert"), None),
        P("expert", None, None),
        P("expert", None, None),
        P("expert", None, None),
    )
    return jax.shard_map(
        body,
        mesh=mesh,
        in_specs=placed,
        out_specs=(
            P(("dp", "expert"), None),
            P(("dp", "expert"), None),
            P("expert", "dp", None),
            P("expert", "dp", None),
            P("expert", None, "dp"),
        ),
        check_vma=False,
    )
```

```python
import functools

import jax
import jax.numpy as jnp
from jax import lax
from jax.experimental import pallas as pl
from jax.experimental.pallas import tpu as pltpu
from jax.sharding import PartitionSpec as P

MESH = pl.DeviceIdType.MESH
F32 = jnp.float32
BF16 = jnp.bfloat16


def tile_of(size, most):
    step = min(size, most)
    while size % step:
        step -= 128
    return step


def paired(index, step, count):
    total, digit = 0, 1
    while digit < count:
        total = total + digit * lax.rem(lax.div(index, digit) + step // digit, 2)
        digit *= 2
    return total


def dot_nt(left, right):
    return lax.dot_general(left, right, (((1,), (1,)), ((), ())), preferred_element_type=F32)


def dot_tn(left, right):
    return lax.dot_general(left, right, (((0,), (0,)), ((), ())), preferred_element_type=F32)


def layer_kernel(
    owners, groups, capacity,
    ids_ref, gates_ref, tok_ref, cot_ref, wg_hbm, wu_hbm, wd_hbm,
    gtok_ref, ggate_ref, gwg_ref, gwu_ref, gwd_ref,
    wg, wu, wd, w_sem,
    pick, gate_col, send_tok, send_cot, rows, scaled, pre_gate, pre_up, score,
    x_rows, x_scaled, x_hid, x_gg, x_gu, own_sem,
    back_send, back_recv, score_send, score_recv, acc_gate, acc_up,
    tok_s, tok_r, cot_s, cot_r, back_s, back_r, sc_s, sc_r,
    fr_s, fr_r, fc_s, fc_r, h_s, h_r, gg_s, gg_r, gu_s, gu_r,
):
    me = lax.axis_index("expert")
    grp = lax.axis_index("dp")
    tok_count, width = tok_ref.shape
    slots = owners * capacity
    hid_width = wg.shape[1]
    part = width // groups
    hid_tile = tile_of(hid_width, 256)
    wide_tile = tile_of(width, 512)

    weight_copies = [
        pltpu.make_async_copy(src.at[0], dst, w_sem.at[i])
        for i, (src, dst) in enumerate(((wg_hbm, wg), (wu_hbm, wu), (wd_hbm, wd)))
    ]
    for copy in weight_copies:
        copy.start()

    barrier = pltpu.get_barrier_semaphore()
    for k in range(1, owners):
        pl.semaphore_signal(
            barrier, inc=1, device_id={"expert": paired(me, k, owners)}, device_id_type=MESH
        )
    for j in range(1, groups):
        pl.semaphore_signal(
            barrier, inc=1, device_id={"dp": paired(grp, j, groups)}, device_id_type=MESH
        )

    expert_no = lax.broadcasted_iota(jnp.int32, (owners, tok_count), 0)
    first = ids_ref[0:1, :] == expert_no
    second = ids_ref[1:2, :] == expert_no
    named = jnp.where(first, 1.0, 0.0) + jnp.where(second, 1.0, 0.0)
    gate_of = jnp.where(first, gates_ref[0:1, :], 0.0) + jnp.where(second, gates_ref[1:2, :], 0.0)
    earlier = jnp.where(
        lax.broadcasted_iota(jnp.int32, (tok_count, tok_count), 0)
        < lax.broadcasted_iota(jnp.int32, (tok_count, tok_count), 1),
        1.0, 0.0,
    ).astype(BF16)
    position = jnp.dot(named.astype(BF16), earlier, preferred_element_type=F32)
    position = jnp.where(named > 0.5, position, -1.0)
    slot_no = lax.broadcasted_iota(jnp.int32, (capacity, tok_count), 0).astype(F32)
    for e in range(owners):
        chosen = jnp.where(slot_no == position[e:e + 1, :], 1.0, 0.0)
        pick[e * capacity:(e + 1) * capacity, :] = chosen.astype(BF16)
        gate_col[e * capacity:(e + 1) * capacity, :] = jnp.broadcast_to(
            jnp.sum(chosen * gate_of[e:e + 1, :], axis=1, keepdims=True), (capacity, 128)
        )

    @pl.loop(0, width // wide_tile)
    def _(n):
        cols = pl.ds(pl.multiple_of(n * wide_tile, wide_tile), wide_tile)
        picked = jnp.dot(pick[...], tok_ref[:, cols], preferred_element_type=F32)
        send_tok[:, :, cols] = picked.astype(BF16).reshape(owners, capacity, wide_tile)

    pl.semaphore_wait(barrier, owners - 1 + groups - 1)

    def across(src, dst, send, recv, k):
        return pltpu.make_async_remote_copy(
            src_ref=src, dst_ref=dst, send_sem=send, recv_sem=recv,
            device_id={"expert": paired(me, k, owners)}, device_id_type=MESH,
        )

    def aside(src, dst, send, recv, j):
        return pltpu.make_async_remote_copy(
            src_ref=src, dst_ref=dst, send_sem=send, recv_sem=recv,
            device_id={"dp": paired(grp, j, groups)}, device_id_type=MESH,
        )

    def send_block(sent, held, send, recv, k):
        return across(sent.at[paired(me, k, owners)], held.at[me], send.at[k], recv.at[k], k)

    def take_block(sent, held, send, recv, k):
        source = paired(me, k, owners)
        across(sent.at[source], held.at[source], send.at[k], recv.at[k], k).wait_recv()
        return source

    def share(held, parts, send, recv, k, j):
        source = paired(me, k, owners)
        target = paired(grp, j, groups)
        cols = pl.ds(pl.multiple_of(target * part, part), part)
        return aside(
            held.at[source, :, cols], parts.at[grp, source], send.at[k, j], recv.at[k, j], j
        )

    def take_share(held, parts, send, recv, k, j):
        source = paired(me, k, owners)
        origin = paired(grp, j, groups)
        aside(
            held.at[source, :, pl.ds(0, part)], parts.at[origin, source],
            send.at[k, j], recv.at[k, j], j,
        ).wait_recv()

    def spread(held, send, recv, j):
        return aside(held.at[grp], held.at[grp], send.at[j], recv.at[j], j)

    def take_spread(held, send, recv, j):
        origin = paired(grp, j, groups)
        aside(held.at[origin], held.at[origin], send.at[j], recv.at[j], j).wait_recv()
        return origin

    def hand_on(held, send, recv, j):
        half = slots // 2
        source = paired(grp, j, groups)
        lines = pl.ds((j - 1) * half, half)
        block = held.at[source, lines]
        return aside(block, block, send.at[3 * (2 - j)], recv.at[3 * (2 - j)], 3 - j)

    def take_on(held, send, recv, j):
        half = slots // 2
        block = held.at[paired(grp, 3, groups), pl.ds((j - 1) * half, half)]
        aside(block, block, send.at[3 * (2 - j)], recv.at[3 * (2 - j)], 3 - j).wait_recv()

    far_first = range(owners - 1, 0, -1)
    for k in far_first:
        send_block(send_tok, rows, tok_s, tok_r, k).start()

    @pl.loop(0, width // wide_tile)
    def _(n):
        cols = pl.ds(pl.multiple_of(n * wide_tile, wide_tile), wide_tile)
        picked = jnp.dot(pick[...], cot_ref[:, cols], preferred_element_type=F32)
        picked = picked * gate_col[:, 0:1]
        send_cot[:, :, cols] = picked.astype(BF16).reshape(owners, capacity, wide_tile)

    rows[me] = send_tok[me]
    scaled[me] = send_cot[me]
    for j in range(1, groups):
        share(rows, x_rows, fr_s, fr_r, 0, j).start()
    for k in far_first:
        send_block(send_tok, rows, tok_s, tok_r, k).wait_send()
        send_block(send_cot, scaled, cot_s, cot_r, k).start()
        take_block(send_tok, rows, tok_s, tok_r, k)
        for j in range(1, groups):
            share(rows, x_rows, fr_s, fr_r, k, j).start()

    mine = pl.ds(pl.multiple_of(grp * part, part), part)
    own_rows = pltpu.make_async_copy(rows.at[:, :, mine], x_rows.at[grp], own_sem.at[0])
    own_rows.start()
    weight_copies[0].wait()
    weight_copies[1].wait()

    @pl.loop(0, hid_width // hid_tile)
    def _(n):
        cols = pl.ds(pl.multiple_of(n * hid_tile, hid_tile), hid_tile)
        held = rows[...].reshape(slots, width)
        gate = jnp.dot(held, wg[:, cols], preferred_element_type=F32)
        up = jnp.dot(held, wu[:, cols], preferred_element_type=F32)
        pre_gate[:, cols] = gate
        pre_up[:, cols] = up
        x_hid[grp, :, cols] = (gate * jax.nn.sigmoid(gate) * up).astype(BF16)

    for j in (1, 2):
        spread(x_hid, h_s, h_r, j).start()
    for j in range(1, groups):
        share(scaled, x_scaled, fc_s, fc_r, 0, j).start()
    for k in far_first:
        take_block(send_cot, scaled, cot_s, cot_r, k)
        for j in range(1, groups):
            share(scaled, x_scaled, fc_s, fc_r, k, j).start()
        if k == owners // 2:
            for j in (1, 2):
                take_spread(x_hid, h_s, h_r, j)
                hand_on(x_hid, h_s, h_r, j).start()
    own_scaled = pltpu.make_async_copy(scaled.at[:, :, mine], x_scaled.at[grp], own_sem.at[1])
    own_scaled.start()
    weight_copies[2].wait()
    score[...] = jnp.zeros_like(score)

    @pl.loop(0, hid_width // hid_tile)
    def _(n):
        cols = pl.ds(pl.multiple_of(n * hid_tile, hid_tile), hid_tile)
        grad_hidden = dot_nt(scaled[...].reshape(slots, width), wd[cols, :])
        gate = pre_gate[:, cols]
        sig = jax.nn.sigmoid(gate)
        x_gg[grp, :, cols] = (
            grad_hidden * pre_up[:, cols] * sig * (1.0 + gate * (1.0 - sig))
        ).astype(BF16)
        x_gu[grp, :, cols] = (grad_hidden * (gate * sig)).astype(BF16)
        score[...] += jnp.broadcast_to(
            jnp.sum(x_hid[grp, :, cols].astype(F32) * grad_hidden, axis=1, keepdims=True),
            (slots, 128),
        )

    for j in (1, 2):
        spread(x_gg, gg_s, gg_r, j).start()
    for j in (1, 2):
        spread(x_gu, gu_s, gu_r, j).start()

    @pl.loop(0, width // wide_tile)
    def _(n):
        cols = pl.ds(pl.multiple_of(n * wide_tile, wide_tile), wide_tile)
        grad = dot_nt(x_gg[grp], wg[cols, :]) + dot_nt(x_gu[grp], wu[cols, :])
        back_send[:, :, cols] = grad.astype(BF16).reshape(owners, capacity, wide_tile)

    on_diagonal = lax.broadcasted_iota(jnp.int32, (capacity, 128), 0) == lax.broadcasted_iota(
        jnp.int32, (capacity, 128), 1
    )
    for e in range(owners):
        line = jnp.sum(
            jnp.where(on_diagonal, score[e * capacity:(e + 1) * capacity, :], 0.0),
            axis=0, keepdims=True,
        )
        score_send[e] = jnp.broadcast_to(line, (8, 128))
    for k in far_first:
        send_block(back_send, back_recv, back_s, back_r, k).start()
        send_block(score_send, score_recv, sc_s, sc_r, k).start()
    back_recv[me] = back_send[me]
    score_recv[me] = score_send[me]

    own_rows.wait()
    own_scaled.wait()
    for j in (1, 2):
        take_on(x_hid, h_s, h_r, j)
    for j in range(1, groups):
        for k in range(owners):
            take_share(rows, x_rows, fr_s, fr_r, k, j)
            take_share(scaled, x_scaled, fc_s, fc_r, k, j)

    @pl.loop(0, hid_width // hid_tile)
    def _(n):
        cols = pl.ds(pl.multiple_of(n * hid_tile, hid_tile), hid_tile)
        gwd_ref[cols, :] = dot_tn(
            x_hid[:, :, cols].reshape(groups * slots, hid_tile),
            x_scaled[...].reshape(groups * slots, part),
        ).astype(BF16)

    def add_group(origin, begin, end):
        @pl.loop(0, hid_width // hid_tile)
        def _(n):
            cols = pl.ds(pl.multiple_of(n * hid_tile, hid_tile), hid_tile)
            left = x_rows[origin].reshape(slots, part)
            gate = dot_tn(left, x_gg[origin, :, cols])
            up = dot_tn(left, x_gu[origin, :, cols])
            if not begin:
                gate = gate + acc_gate[:, cols]
                up = up + acc_up[:, cols]
            if end:
                gwg_ref[:, cols] = gate.astype(BF16)
                gwu_ref[:, cols] = up.astype(BF16)
            else:
                acc_gate[:, cols] = gate
                acc_up[:, cols] = up

    add_group(grp, True, False)
    for j in (1, 2):
        take_spread(x_gg, gg_s, gg_r, j)
        hand_on(x_gg, gg_s, gg_r, j).start()
    for j in (1, 2):
        origin = take_spread(x_gu, gu_s, gu_r, j)
        hand_on(x_gu, gu_s, gu_r, j).start()
        add_group(origin, False, False)

    for k in range(1, owners):
        take_block(back_send, back_recv, back_s, back_r, k)
        take_block(score_send, score_recv, sc_s, sc_r, k)

    @pl.loop(0, width // wide_tile)
    def _(n):
        cols = pl.ds(pl.multiple_of(n * wide_tile, wide_tile), wide_tile)
        gtok_ref[:, cols] = dot_tn(
            pick[...], back_recv[:, :, cols].reshape(slots, wide_tile)
        ).astype(BF16)

    first_sum = jnp.zeros((1, tok_count), F32)
    second_sum = jnp.zeros((1, tok_count), F32)
    for e in range(owners):
        column = jnp.sum(
            jnp.where(on_diagonal, jnp.broadcast_to(score_recv[e, 0:1, :], (capacity, 128)), 0.0),
            axis=1, keepdims=True,
        )
        by_token = jnp.sum(
            pick[e * capacity:(e + 1) * capacity, :].astype(F32) * column, axis=0, keepdims=True
        )
        first_sum = first_sum + jnp.where(ids_ref[0:1, :] == e, by_token, 0.0)
        second_sum = second_sum + jnp.where(ids_ref[1:2, :] == e, by_token, 0.0)
    ggate_ref[0:1, :] = first_sum / gates_ref[0:1, :]
    ggate_ref[1:2, :] = second_sum / gates_ref[1:2, :]

    for j in (1, 2):
        take_on(x_gg, gg_s, gg_r, j)
        take_on(x_gu, gu_s, gu_r, j)
    add_group(paired(grp, 3, groups), False, True)

    for k in range(1, owners):
        send_block(send_cot, scaled, cot_s, cot_r, k).wait_send()
        send_block(back_send, back_recv, back_s, back_r, k).wait_send()
        send_block(score_send, score_recv, sc_s, sc_r, k).wait_send()
    for j in (1, 2):
        for held, send, recv in ((x_hid, h_s, h_r), (x_gg, gg_s, gg_r), (x_gu, gu_s, gu_r)):
            spread(held, send, recv, j).wait_send()
            hand_on(held, send, recv, j).wait_send()
    for j in range(1, groups):
        for k in range(owners):
            share(rows, x_rows, fr_s, fr_r, k, j).wait_send()
            share(scaled, x_scaled, fc_s, fc_r, k, j).wait_send()


def hand_over(*refs):
    count = (len(refs) - 1) // 2
    copies = [
        pltpu.make_async_copy(refs[i], refs[count + i], refs[-1].at[i]) for i in range(count)
    ]
    for copy in copies:
        copy.start()
    for copy in copies:
        copy.wait()


def kernel_body(tokens, expert_ids, gates, cotangent, w_gate, w_up, w_down):
    tok_rows, width = tokens.shape
    owners = lax.axis_size("expert")
    groups = lax.axis_size("dp")
    capacity = slots_of(tok_rows, expert_ids.shape[1], owners)
    hid_width = w_gate.shape[2]
    part = width // groups
    slots = owners * capacity
    vmem = pl.BlockSpec(memory_space=pltpu.VMEM)
    dma = pltpu.SemaphoreType.DMA
    blocks = pltpu.VMEM((owners, capacity, width), BF16)
    parts = pltpu.VMEM((groups, owners, capacity, part), BF16)
    hids = pltpu.VMEM((groups, slots, hid_width), BF16)
    lines = pltpu.VMEM((owners, 8, 128), F32)
    per_owner, per_group, per_share = dma((owners,)), dma((groups,)), dma((owners, groups))
    grad_tokens, grad_gates, grad_gate, grad_up, grad_down = pl.pallas_call(
        functools.partial(layer_kernel, owners, groups, capacity),
        out_shape=(
            jax.ShapeDtypeStruct((tok_rows, width), BF16),
            jax.ShapeDtypeStruct((2, tok_rows), F32),
            jax.ShapeDtypeStruct((part, hid_width), BF16),
            jax.ShapeDtypeStruct((part, hid_width), BF16),
            jax.ShapeDtypeStruct((hid_width, part), BF16),
        ),
        in_specs=[vmem] * 4 + [pl.BlockSpec(memory_space=pl.ANY)] * 3,
        out_specs=(vmem,) * 5,
        scratch_shapes=[
            pltpu.VMEM((width, hid_width), BF16),
            pltpu.VMEM((width, hid_width), BF16),
            pltpu.VMEM((hid_width, width), BF16),
            dma((3,)),
            pltpu.VMEM((slots, tok_rows), BF16),
            pltpu.VMEM((slots, 128), F32),
            blocks, blocks, blocks, blocks,
            pltpu.VMEM((slots, hid_width), F32),
            pltpu.VMEM((slots, hid_width), F32),
            pltpu.VMEM((slots, 128), F32),
            parts, parts, hids, hids, hids,
            dma((2,)),
            blocks, blocks, lines, lines,
            pltpu.VMEM((part, hid_width), F32),
            pltpu.VMEM((part, hid_width), F32),
        ]
        + [per_owner] * 8 + [per_share] * 4 + [per_group] * 6,
        compiler_params=pltpu.CompilerParams(
            collective_id=0, has_side_effects=True, vmem_limit_bytes=56 * 1024 * 1024
        ),
        cost_estimate=pl.CostEstimate(
            flops=16 * slots * width * hid_width,
            bytes_accessed=6 * width * hid_width * 2,
            transcendentals=2 * slots * hid_width,
        ),
        name="expert_layer",
    )(
        expert_ids.T, gates.astype(F32).T, tokens, cotangent, w_gate, w_up, w_down
    )
    held = (grad_tokens, grad_gate[None], grad_up[None], grad_down[None])
    anywhere = pl.BlockSpec(memory_space=pl.ANY)
    grad_tokens, grad_gate, grad_up, grad_down = pl.pallas_call(
        hand_over,
        out_shape=tuple(jax.ShapeDtypeStruct(x.shape, x.dtype) for x in held),
        in_specs=[anywhere] * len(held),
        out_specs=(anywhere,) * len(held),
        scratch_shapes=[dma((len(held),))],
        name="hand_over",
    )(*held)
    return (grad_tokens, grad_gates.T.astype(BF16), grad_gate, grad_up, grad_down)


def contract_rows(left, right):
    return lax.dot_general(
        left, right, (((0,), (0,)), ((), ())), preferred_element_type=jnp.float32
    )


def expert_pass(rows, cot_rows, gate_column, gate_mat, up_mat, down_mat):
    pre_gate = jnp.dot(rows, gate_mat, preferred_element_type=jnp.float32)
    pre_up = jnp.dot(rows, up_mat, preferred_element_type=jnp.float32)
    sigmoid_gate = jax.nn.sigmoid(pre_gate)
    activated = pre_gate * sigmoid_gate
    hidden = (activated * pre_up).astype(jnp.bfloat16)
    expert_out = jnp.dot(hidden, down_mat, preferred_element_type=jnp.float32)
    cot_float = cot_rows.astype(jnp.float32)
    score_grad = jnp.sum(expert_out * cot_float, axis=1)
    scaled = (gate_column.astype(jnp.float32)[:, None] * cot_float).astype(jnp.bfloat16)
    grad_hidden = jnp.dot(scaled, down_mat.T, preferred_element_type=jnp.float32)
    grad_pre_gate = (
        grad_hidden * pre_up * sigmoid_gate * (1.0 + pre_gate * (1.0 - sigmoid_gate))
    ).astype(jnp.bfloat16)
    grad_pre_up = (grad_hidden * activated).astype(jnp.bfloat16)
    row_grad = (
        jnp.dot(grad_pre_gate, gate_mat.T, preferred_element_type=jnp.float32)
        + jnp.dot(grad_pre_up, up_mat.T, preferred_element_type=jnp.float32)
    ).astype(jnp.bfloat16)
    return (hidden, scaled, grad_pre_gate, grad_pre_up, row_grad, score_grad)


def by_owner(values, owners, capacity):
    return values.reshape((owners, capacity) + values.shape[1:])


def sum_weights(part_gate, part_up, part_down):
    return (
        lax.psum_scatter(
            part_gate.astype(jnp.bfloat16), "dp", scatter_dimension=0, tiled=True
        ).astype(jnp.float32),
        lax.psum_scatter(
            part_up.astype(jnp.bfloat16), "dp", scatter_dimension=0, tiled=True
        ).astype(jnp.float32),
        lax.psum_scatter(
            part_down.astype(jnp.bfloat16), "dp", scatter_dimension=1, tiled=True
        ).astype(jnp.float32),
    )


def send_back(row_grad, score_grad, owners, capacity):
    score_half = score_grad.astype(jnp.bfloat16)
    back_rows = lax.all_to_all(
        by_owner(row_grad, owners, capacity), "expert", split_axis=0, concat_axis=0, tiled=True
    )
    back_scores = lax.all_to_all(
        by_owner(score_half, owners, capacity), "expert", split_axis=0, concat_axis=0, tiled=True
    )
    return (back_rows, back_scores)


def plain_body(tokens, expert_ids, gates, cotangent, w_gate, w_up, w_down):
    tok_rows, model_width = tokens.shape
    top_count = expert_ids.shape[1]
    owners = lax.axis_size("expert")
    capacity = min(tok_rows, 3 * tok_rows * top_count // (2 * owners))
    slot_count = owners * capacity
    flat_ids = expert_ids.reshape(-1)
    pair_count = flat_ids.shape[0]
    picked = (flat_ids[:, None] == jnp.arange(owners, dtype=jnp.int32)[None, :]).astype(jnp.int32)
    before = jnp.cumsum(picked, axis=0) - picked
    position = jnp.sum(before * picked, axis=1)
    target = flat_ids * capacity + position
    source_row = jnp.arange(pair_count, dtype=jnp.int32) // top_count
    send_rows = (
        jnp.zeros((slot_count, model_width), jnp.bfloat16).at[target].set(tokens[source_row])
    )
    send_cot = (
        jnp.zeros((slot_count, model_width), jnp.bfloat16).at[target].set(cotangent[source_row])
    )
    send_gate = jnp.zeros((slot_count,), jnp.bfloat16).at[target].set(gates.reshape(-1))
    recv_gate = lax.all_to_all(
        by_owner(send_gate, owners, capacity), "expert", split_axis=0, concat_axis=0, tiled=True
    )
    recv_rows = lax.all_to_all(
        by_owner(send_rows, owners, capacity), "expert", split_axis=0, concat_axis=0, tiled=True
    )
    recv_cot = lax.all_to_all(
        by_owner(send_cot, owners, capacity), "expert", split_axis=0, concat_axis=0, tiled=True
    )
    rows = recv_rows.reshape(slot_count, model_width)
    cot_rows = recv_cot.reshape(slot_count, model_width)
    gate_column = recv_gate.reshape(slot_count)
    hidden, scaled, grad_pre_gate, grad_pre_up, row_grad, score_grad = expert_pass(
        rows, cot_rows, gate_column, w_gate[0], w_up[0], w_down[0]
    )
    part_gate = contract_rows(rows, grad_pre_gate)
    part_up = contract_rows(rows, grad_pre_up)
    part_down = contract_rows(hidden, scaled)
    back_rows, back_scores = send_back(row_grad, score_grad, owners, capacity)
    summed = sum_weights(part_gate, part_up, part_down)
    pair_rows = back_rows.reshape(slot_count, model_width)[target].reshape(
        tok_rows, top_count, model_width
    )
    grad_tokens = jnp.sum(pair_rows.astype(jnp.float32), axis=1).astype(jnp.bfloat16)
    grad_gates = back_scores.reshape(slot_count)[target].reshape(tok_rows, top_count)
    grad_w_gate = summed[0].astype(jnp.bfloat16)[None]
    grad_w_up = summed[1].astype(jnp.bfloat16)[None]
    grad_w_down = summed[2].astype(jnp.bfloat16)[None]
    return (grad_tokens, grad_gates, grad_w_gate, grad_w_up, grad_w_down)


def slots_of(tok_rows, top_count, owners):
    return min(tok_rows, 3 * tok_rows * top_count // (2 * owners))


def body(tokens, expert_ids, gates, cotangent, w_gate, w_up, w_down):
    capacity = slots_of(tokens.shape[0], expert_ids.shape[1], lax.axis_size("expert"))
    even = lax.axis_size("dp") == 4 and lax.axis_size("expert") == 8
    chosen = kernel_body if even and capacity % 16 == 0 else plain_body
    return chosen(tokens, expert_ids, gates, cotangent, w_gate, w_up, w_down)


def solution(mesh):
    placed = (
        P(("dp", "expert"), None),
        P(("dp", "expert"), None),
        P(("dp", "expert"), None),
        P(("dp", "expert"), None),
        P("expert", None, None),
        P("expert", None, None),
        P("expert", None, None),
    )
    return jax.shard_map(
        body,
        mesh=mesh,
        in_specs=placed,
        out_specs=(
            P(("dp", "expert"), None),
            P(("dp", "expert"), None),
            P("expert", "dp", None),
            P("expert", "dp", None),
            P("expert", None, "dp"),
        ),
        check_vma=False,
    )
```

```python
import functools

import jax
import jax.numpy as jnp
from jax import lax
from jax.experimental import pallas as pl
from jax.experimental.pallas import tpu as pltpu
from jax.sharding import PartitionSpec as P

MESH = pl.DeviceIdType.MESH
F32 = jnp.float32
BF16 = jnp.bfloat16


def tile_of(size, most):
    step = min(size, most)
    while size % step:
        step -= 128
    return step


def paired(index, step, count):
    total, digit = 0, 1
    while digit < count:
        total = total + digit * lax.rem(lax.div(index, digit) + lax.div(step, digit), 2)
        digit *= 2
    return total


def dot_nt(left, right):
    return lax.dot_general(left, right, (((1,), (1,)), ((), ())), preferred_element_type=F32)


def dot_tn(left, right):
    return lax.dot_general(left, right, (((0,), (0,)), ((), ())), preferred_element_type=F32)


def layer_kernel(
    owners, groups, capacity,
    ids_ref, gates_ref, tok_ref, cot_ref, wg_hbm, wu_hbm, wd_hbm,
    gtok_ref, ggate_ref, gwg_ref, gwu_ref, gwd_ref,
    wg, wu, wd, w_sem,
    pick, gate_col, send_tok, send_cot, rows, scaled, pre_gate, pre_up, score,
    x_rows, x_scaled, x_hid, x_gg, x_gu, own_sem,
    back_send, back_recv, score_send, score_recv, acc_gate, acc_up,
    tok_s, tok_r, cot_s, cot_r, back_s, back_r, sc_s, sc_r,
    fr_s, fr_r, fc_s, fc_r, h_s, h_r, gg_s, gg_r, gu_s, gu_r,
):
    me = lax.axis_index("expert")
    grp = lax.axis_index("dp")
    tok_count, width = tok_ref.shape
    slots = owners * capacity
    hid_width = wg.shape[1]
    part = width // groups
    hid_tile = tile_of(hid_width, 256)
    wide_tile = tile_of(width, 512)

    weight_copies = [
        pltpu.make_async_copy(src.at[0], dst, w_sem.at[i])
        for i, (src, dst) in enumerate(((wg_hbm, wg), (wu_hbm, wu), (wd_hbm, wd)))
    ]
    for copy in weight_copies:
        copy.start()

    barrier = pltpu.get_barrier_semaphore()
    for k in range(1, owners):
        pl.semaphore_signal(
            barrier, inc=1, device_id={"expert": paired(me, k, owners)}, device_id_type=MESH
        )
    for j in range(1, groups):
        pl.semaphore_signal(
            barrier, inc=1, device_id={"dp": paired(grp, j, groups)}, device_id_type=MESH
        )

    expert_no = lax.broadcasted_iota(jnp.int32, (owners, tok_count), 0)
    first = ids_ref[0:1, :] == expert_no
    second = ids_ref[1:2, :] == expert_no
    named = jnp.where(first, 1.0, 0.0) + jnp.where(second, 1.0, 0.0)
    gate_of = jnp.where(first, gates_ref[0:1, :], 0.0) + jnp.where(second, gates_ref[1:2, :], 0.0)
    earlier = jnp.where(
        lax.broadcasted_iota(jnp.int32, (tok_count, tok_count), 0)
        < lax.broadcasted_iota(jnp.int32, (tok_count, tok_count), 1),
        1.0, 0.0,
    ).astype(BF16)
    position = jnp.dot(named.astype(BF16), earlier, preferred_element_type=F32)
    position = jnp.where(named > 0.5, position, -1.0)
    slot_no = lax.broadcasted_iota(jnp.int32, (capacity, tok_count), 0).astype(F32)
    for e in range(owners):
        chosen = jnp.where(slot_no == position[e:e + 1, :], 1.0, 0.0)
        pick[e * capacity:(e + 1) * capacity, :] = chosen.astype(BF16)
        gate_col[e * capacity:(e + 1) * capacity, :] = jnp.broadcast_to(
            jnp.sum(chosen * gate_of[e:e + 1, :], axis=1, keepdims=True), (capacity, 128)
        )

    @pl.loop(0, width // wide_tile)
    def _(n):
        cols = pl.ds(pl.multiple_of(n * wide_tile, wide_tile), wide_tile)
        picked = jnp.dot(pick[...], tok_ref[:, cols], preferred_element_type=F32)
        send_tok[:, :, cols] = picked.astype(BF16).reshape(owners, capacity, wide_tile)

    pl.semaphore_wait(barrier, owners - 1 + groups - 1)

    def across(src, dst, send, recv, k):
        return pltpu.make_async_remote_copy(
            src_ref=src, dst_ref=dst, send_sem=send, recv_sem=recv,
            device_id={"expert": paired(me, k, owners)}, device_id_type=MESH,
        )

    def aside(src, dst, send, recv, j):
        return pltpu.make_async_remote_copy(
            src_ref=src, dst_ref=dst, send_sem=send, recv_sem=recv,
            device_id={"dp": paired(grp, j, groups)}, device_id_type=MESH,
        )

    def send_block(sent, held, send, recv, k):
        return across(sent.at[paired(me, k, owners)], held.at[me], send.at[k], recv.at[k], k)

    def take_block(sent, held, send, recv, k):
        source = paired(me, k, owners)
        across(sent.at[source], held.at[source], send.at[k], recv.at[k], k).wait_recv()
        return source

    def share(held, parts, send, recv, k, j):
        source = paired(me, k, owners)
        target = paired(grp, j, groups)
        cols = pl.ds(pl.multiple_of(target * part, part), part)
        return aside(
            held.at[source, :, cols], parts.at[grp, source], send.at[k, j], recv.at[k, j], j
        )

    def take_share(held, parts, send, recv, k, j):
        source = paired(me, k, owners)
        origin = paired(grp, j, groups)
        aside(
            held.at[source, :, pl.ds(0, part)], parts.at[origin, source],
            send.at[k, j], recv.at[k, j], j,
        ).wait_recv()

    def spread(held, send, recv, j):
        return aside(held.at[grp], held.at[grp], send.at[j], recv.at[j], j)

    def take_spread(held, send, recv, j):
        origin = paired(grp, j, groups)
        aside(held.at[origin], held.at[origin], send.at[j], recv.at[j], j).wait_recv()
        return origin

    def hand_on(held, send, recv, j):
        half = slots // 2
        source = paired(grp, j, groups)
        lines = pl.ds((j - 1) * half, half)
        block = held.at[source, lines]
        return aside(block, block, send.at[3 * (2 - j)], recv.at[3 * (2 - j)], 3 - j)

    def take_on(held, send, recv, j):
        half = slots // 2
        block = held.at[paired(grp, 3, groups), pl.ds((j - 1) * half, half)]
        aside(block, block, send.at[3 * (2 - j)], recv.at[3 * (2 - j)], 3 - j).wait_recv()

    chip = lax.div(me, 2)
    inner = lax.rem(lax.div(chip + 1, 2), 2)
    out_order, in_order = [1], [1]
    for i in range(3):
        for core in range(2):
            out_order.append(2 * (1 + lax.rem(i + inner, 3)) + core)
            in_order.append(2 * (1 + lax.rem(i + 1 - inner, 3)) + core)
    for k in out_order:
        send_block(send_tok, rows, tok_s, tok_r, k).start()

    @pl.loop(0, width // wide_tile)
    def _(n):
        cols = pl.ds(pl.multiple_of(n * wide_tile, wide_tile), wide_tile)
        picked = jnp.dot(pick[...], cot_ref[:, cols], preferred_element_type=F32)
        picked = picked * gate_col[:, 0:1]
        send_cot[:, :, cols] = picked.astype(BF16).reshape(owners, capacity, wide_tile)

    rows[me] = send_tok[me]
    scaled[me] = send_cot[me]
    for j in range(1, groups):
        share(rows, x_rows, fr_s, fr_r, 0, j).start()
    for out, k in zip(out_order, in_order):
        send_block(send_tok, rows, tok_s, tok_r, out).wait_send()
        send_block(send_cot, scaled, cot_s, cot_r, out).start()
        take_block(send_tok, rows, tok_s, tok_r, k)
        for j in range(1, groups):
            share(rows, x_rows, fr_s, fr_r, k, j).start()

    mine = pl.ds(pl.multiple_of(grp * part, part), part)
    own_rows = pltpu.make_async_copy(rows.at[:, :, mine], x_rows.at[grp], own_sem.at[0])
    own_rows.start()
    weight_copies[0].wait()
    weight_copies[1].wait()

    @pl.loop(0, hid_width // hid_tile)
    def _(n):
        cols = pl.ds(pl.multiple_of(n * hid_tile, hid_tile), hid_tile)
        held = rows[...].reshape(slots, width)
        gate = jnp.dot(held, wg[:, cols], preferred_element_type=F32)
        up = jnp.dot(held, wu[:, cols], preferred_element_type=F32)
        pre_gate[:, cols] = gate
        pre_up[:, cols] = up
        x_hid[grp, :, cols] = (gate * jax.nn.sigmoid(gate) * up).astype(BF16)

    for j in (1, 2):
        spread(x_hid, h_s, h_r, j).start()
    for j in range(1, groups):
        share(scaled, x_scaled, fc_s, fc_r, 0, j).start()
    for step, k in enumerate(in_order):
        take_block(send_cot, scaled, cot_s, cot_r, k)
        for j in range(1, groups):
            share(scaled, x_scaled, fc_s, fc_r, k, j).start()
        if step == owners // 2:
            for j in (1, 2):
                take_spread(x_hid, h_s, h_r, j)
                hand_on(x_hid, h_s, h_r, j).start()
    own_scaled = pltpu.make_async_copy(scaled.at[:, :, mine], x_scaled.at[grp], own_sem.at[1])
    own_scaled.start()
    weight_copies[2].wait()
    score[...] = jnp.zeros_like(score)

    @pl.loop(0, hid_width // hid_tile)
    def _(n):
        cols = pl.ds(pl.multiple_of(n * hid_tile, hid_tile), hid_tile)
        grad_hidden = dot_nt(scaled[...].reshape(slots, width), wd[cols, :])
        gate = pre_gate[:, cols]
        sig = jax.nn.sigmoid(gate)
        x_gg[grp, :, cols] = (
            grad_hidden * pre_up[:, cols] * sig * (1.0 + gate * (1.0 - sig))
        ).astype(BF16)
        x_gu[grp, :, cols] = (grad_hidden * (gate * sig)).astype(BF16)
        score[...] += jnp.broadcast_to(
            jnp.sum(x_hid[grp, :, cols].astype(F32) * grad_hidden, axis=1, keepdims=True),
            (slots, 128),
        )

    for j in (1, 2):
        spread(x_gg, gg_s, gg_r, j).start()
    for j in (1, 2):
        spread(x_gu, gu_s, gu_r, j).start()

    @pl.loop(0, width // wide_tile)
    def _(n):
        cols = pl.ds(pl.multiple_of(n * wide_tile, wide_tile), wide_tile)
        grad = dot_nt(x_gg[grp], wg[cols, :]) + dot_nt(x_gu[grp], wu[cols, :])
        back_send[:, :, cols] = grad.astype(BF16).reshape(owners, capacity, wide_tile)

    on_diagonal = lax.broadcasted_iota(jnp.int32, (capacity, 128), 0) == lax.broadcasted_iota(
        jnp.int32, (capacity, 128), 1
    )
    for e in range(owners):
        line = jnp.sum(
            jnp.where(on_diagonal, score[e * capacity:(e + 1) * capacity, :], 0.0),
            axis=0, keepdims=True,
        )
        score_send[e] = jnp.broadcast_to(line, (8, 128))
    for k in out_order:
        send_block(back_send, back_recv, back_s, back_r, k).start()
        send_block(score_send, score_recv, sc_s, sc_r, k).start()
    back_recv[me] = back_send[me]
    score_recv[me] = score_send[me]

    own_rows.wait()
    own_scaled.wait()
    for j in (1, 2):
        take_on(x_hid, h_s, h_r, j)
    for j in range(1, groups):
        for k in range(owners):
            take_share(rows, x_rows, fr_s, fr_r, k, j)
            take_share(scaled, x_scaled, fc_s, fc_r, k, j)

    @pl.loop(0, hid_width // hid_tile)
    def _(n):
        cols = pl.ds(pl.multiple_of(n * hid_tile, hid_tile), hid_tile)
        gwd_ref[cols, :] = dot_tn(
            x_hid[:, :, cols].reshape(groups * slots, hid_tile),
            x_scaled[...].reshape(groups * slots, part),
        ).astype(BF16)

    def add_group(origin, begin, end):
        @pl.loop(0, hid_width // hid_tile)
        def _(n):
            cols = pl.ds(pl.multiple_of(n * hid_tile, hid_tile), hid_tile)
            left = x_rows[origin].reshape(slots, part)
            gate = dot_tn(left, x_gg[origin, :, cols])
            up = dot_tn(left, x_gu[origin, :, cols])
            if not begin:
                gate = gate + acc_gate[:, cols]
                up = up + acc_up[:, cols]
            if end:
                gwg_ref[:, cols] = gate.astype(BF16)
                gwu_ref[:, cols] = up.astype(BF16)
            else:
                acc_gate[:, cols] = gate
                acc_up[:, cols] = up

    add_group(grp, True, False)
    for j in (1, 2):
        take_spread(x_gg, gg_s, gg_r, j)
        hand_on(x_gg, gg_s, gg_r, j).start()
    for j in (1, 2):
        origin = take_spread(x_gu, gu_s, gu_r, j)
        hand_on(x_gu, gu_s, gu_r, j).start()
        add_group(origin, False, False)

    for k in range(1, owners):
        take_block(back_send, back_recv, back_s, back_r, k)
        take_block(score_send, score_recv, sc_s, sc_r, k)

    @pl.loop(0, width // wide_tile)
    def _(n):
        cols = pl.ds(pl.multiple_of(n * wide_tile, wide_tile), wide_tile)
        gtok_ref[:, cols] = dot_tn(
            pick[...], back_recv[:, :, cols].reshape(slots, wide_tile)
        ).astype(BF16)

    first_sum = jnp.zeros((1, tok_count), F32)
    second_sum = jnp.zeros((1, tok_count), F32)
    for e in range(owners):
        column = jnp.sum(
            jnp.where(on_diagonal, jnp.broadcast_to(score_recv[e, 0:1, :], (capacity, 128)), 0.0),
            axis=1, keepdims=True,
        )
        by_token = jnp.sum(
            pick[e * capacity:(e + 1) * capacity, :].astype(F32) * column, axis=0, keepdims=True
        )
        first_sum = first_sum + jnp.where(ids_ref[0:1, :] == e, by_token, 0.0)
        second_sum = second_sum + jnp.where(ids_ref[1:2, :] == e, by_token, 0.0)
    ggate_ref[0:1, :] = first_sum / gates_ref[0:1, :]
    ggate_ref[1:2, :] = second_sum / gates_ref[1:2, :]

    for j in (1, 2):
        take_on(x_gg, gg_s, gg_r, j)
        take_on(x_gu, gu_s, gu_r, j)
    add_group(paired(grp, 3, groups), False, True)

    for k in range(1, owners):
        send_block(send_cot, scaled, cot_s, cot_r, k).wait_send()
        send_block(back_send, back_recv, back_s, back_r, k).wait_send()
        send_block(score_send, score_recv, sc_s, sc_r, k).wait_send()
    for j in (1, 2):
        for held, send, recv in ((x_hid, h_s, h_r), (x_gg, gg_s, gg_r), (x_gu, gu_s, gu_r)):
            spread(held, send, recv, j).wait_send()
            hand_on(held, send, recv, j).wait_send()
    for j in range(1, groups):
        for k in range(owners):
            share(rows, x_rows, fr_s, fr_r, k, j).wait_send()
            share(scaled, x_scaled, fc_s, fc_r, k, j).wait_send()


def hand_over(*refs):
    count = len(refs) // 2
    for i in range(count):
        refs[count + i][...] = refs[i][...]


def kernel_body(tokens, expert_ids, gates, cotangent, w_gate, w_up, w_down):
    tok_rows, width = tokens.shape
    owners = lax.axis_size("expert")
    groups = lax.axis_size("dp")
    capacity = slots_of(tok_rows, expert_ids.shape[1], owners)
    hid_width = w_gate.shape[2]
    part = width // groups
    slots = owners * capacity
    vmem = pl.BlockSpec(memory_space=pltpu.VMEM)
    dma = pltpu.SemaphoreType.DMA
    blocks = pltpu.VMEM((owners, capacity, width), BF16)
    parts = pltpu.VMEM((groups, owners, capacity, part), BF16)
    hids = pltpu.VMEM((groups, slots, hid_width), BF16)
    lines = pltpu.VMEM((owners, 8, 128), F32)
    per_owner, per_group, per_share = dma((owners,)), dma((groups,)), dma((owners, groups))
    grad_tokens, grad_gates, grad_gate, grad_up, grad_down = pl.pallas_call(
        functools.partial(layer_kernel, owners, groups, capacity),
        out_shape=(
            jax.ShapeDtypeStruct((tok_rows, width), BF16),
            jax.ShapeDtypeStruct((2, tok_rows), F32),
            jax.ShapeDtypeStruct((part, hid_width), BF16),
            jax.ShapeDtypeStruct((part, hid_width), BF16),
            jax.ShapeDtypeStruct((hid_width, part), BF16),
        ),
        in_specs=[vmem] * 4 + [pl.BlockSpec(memory_space=pl.ANY)] * 3,
        out_specs=(vmem,) * 5,
        scratch_shapes=[
            pltpu.VMEM((width, hid_width), BF16),
            pltpu.VMEM((width, hid_width), BF16),
            pltpu.VMEM((hid_width, width), BF16),
            dma((3,)),
            pltpu.VMEM((slots, tok_rows), BF16),
            pltpu.VMEM((slots, 128), F32),
            blocks, blocks, blocks, blocks,
            pltpu.VMEM((slots, hid_width), F32),
            pltpu.VMEM((slots, hid_width), F32),
            pltpu.VMEM((slots, 128), F32),
            parts, parts, hids, hids, hids,
            dma((2,)),
            blocks, blocks, lines, lines,
            pltpu.VMEM((part, hid_width), F32),
            pltpu.VMEM((part, hid_width), F32),
        ]
        + [per_owner] * 8 + [per_share] * 4 + [per_group] * 6,
        compiler_params=pltpu.CompilerParams(
            collective_id=0, has_side_effects=True, vmem_limit_bytes=56 * 1024 * 1024
        ),
        cost_estimate=pl.CostEstimate(
            flops=16 * slots * width * hid_width,
            bytes_accessed=6 * width * hid_width * 2,
            transcendentals=2 * slots * hid_width,
        ),
        name="expert_layer",
    )(
        expert_ids.T, gates.astype(F32).T, tokens, cotangent, w_gate, w_up, w_down
    )
    held = (grad_tokens, grad_gate[None], grad_up[None], grad_down[None])
    quarters = [
        pl.BlockSpec(
            x.shape[:-2] + (x.shape[-2] // 4, x.shape[-1]),
            (lambda n: (n, 0)) if x.ndim == 2 else (lambda n: (0, n, 0)),
        )
        for x in held
    ]
    grad_tokens, grad_gate, grad_up, grad_down = pl.pallas_call(
        hand_over,
        grid=(4,),
        out_shape=tuple(jax.ShapeDtypeStruct(x.shape, x.dtype) for x in held),
        in_specs=quarters,
        out_specs=tuple(quarters),
        name="hand_over",
    )(*held)
    return (grad_tokens, grad_gates.T.astype(BF16), grad_gate, grad_up, grad_down)


def contract_rows(left, right):
    return lax.dot_general(
        left, right, (((0,), (0,)), ((), ())), preferred_element_type=jnp.float32
    )


def expert_pass(rows, cot_rows, gate_column, gate_mat, up_mat, down_mat):
    pre_gate = jnp.dot(rows, gate_mat, preferred_element_type=jnp.float32)
    pre_up = jnp.dot(rows, up_mat, preferred_element_type=jnp.float32)
    sigmoid_gate = jax.nn.sigmoid(pre_gate)
    activated = pre_gate * sigmoid_gate
    hidden = (activated * pre_up).astype(jnp.bfloat16)
    expert_out = jnp.dot(hidden, down_mat, preferred_element_type=jnp.float32)
    cot_float = cot_rows.astype(jnp.float32)
    score_grad = jnp.sum(expert_out * cot_float, axis=1)
    scaled = (gate_column.astype(jnp.float32)[:, None] * cot_float).astype(jnp.bfloat16)
    grad_hidden = jnp.dot(scaled, down_mat.T, preferred_element_type=jnp.float32)
    grad_pre_gate = (
        grad_hidden * pre_up * sigmoid_gate * (1.0 + pre_gate * (1.0 - sigmoid_gate))
    ).astype(jnp.bfloat16)
    grad_pre_up = (grad_hidden * activated).astype(jnp.bfloat16)
    row_grad = (
        jnp.dot(grad_pre_gate, gate_mat.T, preferred_element_type=jnp.float32)
        + jnp.dot(grad_pre_up, up_mat.T, preferred_element_type=jnp.float32)
    ).astype(jnp.bfloat16)
    return (hidden, scaled, grad_pre_gate, grad_pre_up, row_grad, score_grad)


def by_owner(values, owners, capacity):
    return values.reshape((owners, capacity) + values.shape[1:])


def sum_weights(part_gate, part_up, part_down):
    return (
        lax.psum_scatter(
            part_gate.astype(jnp.bfloat16), "dp", scatter_dimension=0, tiled=True
        ).astype(jnp.float32),
        lax.psum_scatter(
            part_up.astype(jnp.bfloat16), "dp", scatter_dimension=0, tiled=True
        ).astype(jnp.float32),
        lax.psum_scatter(
            part_down.astype(jnp.bfloat16), "dp", scatter_dimension=1, tiled=True
        ).astype(jnp.float32),
    )


def send_back(row_grad, score_grad, owners, capacity):
    score_half = score_grad.astype(jnp.bfloat16)
    back_rows = lax.all_to_all(
        by_owner(row_grad, owners, capacity), "expert", split_axis=0, concat_axis=0, tiled=True
    )
    back_scores = lax.all_to_all(
        by_owner(score_half, owners, capacity), "expert", split_axis=0, concat_axis=0, tiled=True
    )
    return (back_rows, back_scores)


def plain_body(tokens, expert_ids, gates, cotangent, w_gate, w_up, w_down):
    tok_rows, model_width = tokens.shape
    top_count = expert_ids.shape[1]
    owners = lax.axis_size("expert")
    capacity = min(tok_rows, 3 * tok_rows * top_count // (2 * owners))
    slot_count = owners * capacity
    flat_ids = expert_ids.reshape(-1)
    pair_count = flat_ids.shape[0]
    picked = (flat_ids[:, None] == jnp.arange(owners, dtype=jnp.int32)[None, :]).astype(jnp.int32)
    before = jnp.cumsum(picked, axis=0) - picked
    position = jnp.sum(before * picked, axis=1)
    target = flat_ids * capacity + position
    source_row = jnp.arange(pair_count, dtype=jnp.int32) // top_count
    send_rows = (
        jnp.zeros((slot_count, model_width), jnp.bfloat16).at[target].set(tokens[source_row])
    )
    send_cot = (
        jnp.zeros((slot_count, model_width), jnp.bfloat16).at[target].set(cotangent[source_row])
    )
    send_gate = jnp.zeros((slot_count,), jnp.bfloat16).at[target].set(gates.reshape(-1))
    recv_gate = lax.all_to_all(
        by_owner(send_gate, owners, capacity), "expert", split_axis=0, concat_axis=0, tiled=True
    )
    recv_rows = lax.all_to_all(
        by_owner(send_rows, owners, capacity), "expert", split_axis=0, concat_axis=0, tiled=True
    )
    recv_cot = lax.all_to_all(
        by_owner(send_cot, owners, capacity), "expert", split_axis=0, concat_axis=0, tiled=True
    )
    rows = recv_rows.reshape(slot_count, model_width)
    cot_rows = recv_cot.reshape(slot_count, model_width)
    gate_column = recv_gate.reshape(slot_count)
    hidden, scaled, grad_pre_gate, grad_pre_up, row_grad, score_grad = expert_pass(
        rows, cot_rows, gate_column, w_gate[0], w_up[0], w_down[0]
    )
    part_gate = contract_rows(rows, grad_pre_gate)
    part_up = contract_rows(rows, grad_pre_up)
    part_down = contract_rows(hidden, scaled)
    back_rows, back_scores = send_back(row_grad, score_grad, owners, capacity)
    summed = sum_weights(part_gate, part_up, part_down)
    pair_rows = back_rows.reshape(slot_count, model_width)[target].reshape(
        tok_rows, top_count, model_width
    )
    grad_tokens = jnp.sum(pair_rows.astype(jnp.float32), axis=1).astype(jnp.bfloat16)
    grad_gates = back_scores.reshape(slot_count)[target].reshape(tok_rows, top_count)
    grad_w_gate = summed[0].astype(jnp.bfloat16)[None]
    grad_w_up = summed[1].astype(jnp.bfloat16)[None]
    grad_w_down = summed[2].astype(jnp.bfloat16)[None]
    return (grad_tokens, grad_gates, grad_w_gate, grad_w_up, grad_w_down)


def slots_of(tok_rows, top_count, owners):
    return min(tok_rows, 3 * tok_rows * top_count // (2 * owners))


def body(tokens, expert_ids, gates, cotangent, w_gate, w_up, w_down):
    capacity = slots_of(tokens.shape[0], expert_ids.shape[1], lax.axis_size("expert"))
    even = lax.axis_size("dp") == 4 and lax.axis_size("expert") == 8
    chosen = kernel_body if even and capacity % 16 == 0 else plain_body
    return chosen(tokens, expert_ids, gates, cotangent, w_gate, w_up, w_down)


def solution(mesh):
    placed = (
        P(("dp", "expert"), None),
        P(("dp", "expert"), None),
        P(("dp", "expert"), None),
        P(("dp", "expert"), None),
        P("expert", None, None),
        P("expert", None, None),
        P("expert", None, None),
    )
    return jax.shard_map(
        body,
        mesh=mesh,
        in_specs=placed,
        out_specs=(
            P(("dp", "expert"), None),
            P(("dp", "expert"), None),
            P("expert", "dp", None),
            P("expert", "dp", None),
            P("expert", None, "dp"),
        ),
        check_vma=False,
    )
```

```python
import functools

import jax
import jax.numpy as jnp
from jax import lax
from jax.experimental import pallas as pl
from jax.experimental.pallas import tpu as pltpu
from jax.sharding import PartitionSpec as P

MESH = pl.DeviceIdType.MESH
F32 = jnp.float32
BF16 = jnp.bfloat16


def tile_of(size, most):
    step = min(size, most)
    while size % step:
        step -= 128
    return step


def paired(index, step, count):
    total, digit = 0, 1
    while digit < count:
        total = total + digit * lax.rem(lax.div(index, digit) + lax.div(step, digit), 2)
        digit *= 2
    return total


def dot_nt(left, right):
    return lax.dot_general(left, right, (((1,), (1,)), ((), ())), preferred_element_type=F32)


def dot_tn(left, right):
    return lax.dot_general(left, right, (((0,), (0,)), ((), ())), preferred_element_type=F32)


def layer_kernel(
    owners, groups, capacity,
    ids_ref, gates_ref, tok_ref, cot_ref, wg_hbm, wu_hbm, wd_hbm,
    gtok_ref, ggate_ref, gwg_ref, gwu_ref, gwd_ref,
    wg, wu, wd, w_sem,
    pick, gate_col, send_tok, send_cot, rows, scaled, gate_factor, up_factor, score,
    x_rows, x_scaled, x_hid, x_gg, x_gu, own_sem,
    back_send, back_recv, score_send, score_recv, acc_gate, acc_up,
    tok_s, tok_r, cot_s, cot_r, back_s, back_r, sc_s, sc_r,
    fr_s, fr_r, fc_s, fc_r, h_s, h_r, gg_s, gg_r, gu_s, gu_r,
):
    me = lax.axis_index("expert")
    grp = lax.axis_index("dp")
    tok_count, width = tok_ref.shape
    slots = owners * capacity
    hid_width = wg.shape[1]
    part = width // groups
    hid_tile = tile_of(hid_width, 256)
    wide_tile = tile_of(width, 512)

    weight_copies = [
        pltpu.make_async_copy(src.at[0], dst, w_sem.at[i])
        for i, (src, dst) in enumerate(((wg_hbm, wg), (wu_hbm, wu), (wd_hbm, wd)))
    ]
    for copy in weight_copies:
        copy.start()

    barrier = pltpu.get_barrier_semaphore()
    for k in range(1, owners):
        pl.semaphore_signal(
            barrier, inc=1, device_id={"expert": paired(me, k, owners)}, device_id_type=MESH
        )
    for j in range(1, groups):
        pl.semaphore_signal(
            barrier, inc=1, device_id={"dp": paired(grp, j, groups)}, device_id_type=MESH
        )

    expert_no = lax.broadcasted_iota(jnp.int32, (owners, tok_count), 0)
    first = ids_ref[0:1, :] == expert_no
    second = ids_ref[1:2, :] == expert_no
    named = jnp.where(first, 1.0, 0.0) + jnp.where(second, 1.0, 0.0)
    weights = gates_ref[...].astype(F32)
    gate_of = jnp.where(first, weights[0:1, :], 0.0) + jnp.where(second, weights[1:2, :], 0.0)
    earlier = jnp.where(
        lax.broadcasted_iota(jnp.int32, (tok_count, tok_count), 0)
        < lax.broadcasted_iota(jnp.int32, (tok_count, tok_count), 1),
        1.0, 0.0,
    ).astype(BF16)
    position = jnp.dot(named.astype(BF16), earlier, preferred_element_type=F32)
    position = jnp.where(named > 0.5, position, -1.0)
    slot_no = lax.broadcasted_iota(jnp.int32, (capacity, tok_count), 0).astype(F32)
    for e in range(owners):
        chosen = jnp.where(slot_no == position[e:e + 1, :], 1.0, 0.0)
        pick[e * capacity:(e + 1) * capacity, :] = chosen.astype(BF16)
        gate_col[e * capacity:(e + 1) * capacity, :] = jnp.broadcast_to(
            jnp.sum(chosen * gate_of[e:e + 1, :], axis=1, keepdims=True), (capacity, 128)
        )

    @pl.loop(0, width // wide_tile)
    def _(n):
        cols = pl.ds(pl.multiple_of(n * wide_tile, wide_tile), wide_tile)
        picked = jnp.dot(pick[...], tok_ref[:, cols], preferred_element_type=F32)
        send_tok[:, :, cols] = picked.astype(BF16).reshape(owners, capacity, wide_tile)

    pl.semaphore_wait(barrier, owners - 1 + groups - 1)

    def across(src, dst, send, recv, k):
        return pltpu.make_async_remote_copy(
            src_ref=src, dst_ref=dst, send_sem=send, recv_sem=recv,
            device_id={"expert": paired(me, k, owners)}, device_id_type=MESH,
        )

    def aside(src, dst, send, recv, j):
        return pltpu.make_async_remote_copy(
            src_ref=src, dst_ref=dst, send_sem=send, recv_sem=recv,
            device_id={"dp": paired(grp, j, groups)}, device_id_type=MESH,
        )

    def send_block(sent, held, send, recv, k):
        return across(sent.at[paired(me, k, owners)], held.at[me], send.at[k], recv.at[k], k)

    def take_block(sent, held, send, recv, k):
        source = paired(me, k, owners)
        across(sent.at[source], held.at[source], send.at[k], recv.at[k], k).wait_recv()
        return source

    def share(held, parts, send, recv, k, j):
        source = paired(me, k, owners)
        target = paired(grp, j, groups)
        cols = pl.ds(pl.multiple_of(target * part, part), part)
        return aside(
            held.at[source, :, cols], parts.at[grp, source], send.at[k, j], recv.at[k, j], j
        )

    def take_share(held, parts, send, recv, k, j):
        source = paired(me, k, owners)
        origin = paired(grp, j, groups)
        aside(
            held.at[source, :, pl.ds(0, part)], parts.at[origin, source],
            send.at[k, j], recv.at[k, j], j,
        ).wait_recv()

    def spread(held, send, recv, j):
        return aside(held.at[grp], held.at[grp], send.at[j], recv.at[j], j)

    def take_spread(held, send, recv, j):
        origin = paired(grp, j, groups)
        aside(held.at[origin], held.at[origin], send.at[j], recv.at[j], j).wait_recv()
        return origin

    def hand_on(held, send, recv, j):
        half = slots // 2
        source = paired(grp, j, groups)
        lines = pl.ds((j - 1) * half, half)
        block = held.at[source, lines]
        return aside(block, block, send.at[3 * (2 - j)], recv.at[3 * (2 - j)], 3 - j)

    def take_on(held, send, recv, j):
        half = slots // 2
        block = held.at[paired(grp, 3, groups), pl.ds((j - 1) * half, half)]
        aside(block, block, send.at[3 * (2 - j)], recv.at[3 * (2 - j)], 3 - j).wait_recv()

    def tile(n):
        return pl.ds(pl.multiple_of(n * hid_tile, hid_tile), hid_tile)

    def spread_tile(held, send, recv, n, j):
        block = held.at[grp, :, tile(n)]
        return aside(block, block, send.at[n, j], recv.at[n, j], j)

    def take_tile(held, send, recv, n, j):
        block = held.at[paired(grp, j, groups), :, tile(n)]
        aside(block, block, send.at[n, j], recv.at[n, j], j).wait_recv()

    def hand_on_tile(held, send, recv, n, j):
        half = slots // 2
        block = held.at[paired(grp, j, groups), pl.ds((j - 1) * half, half), tile(n)]
        return aside(block, block, send.at[n, 3 * (2 - j)], recv.at[n, 3 * (2 - j)], 3 - j)

    def take_on_tile(held, send, recv, n, j):
        half = slots // 2
        block = held.at[paired(grp, 3, groups), pl.ds((j - 1) * half, half), tile(n)]
        aside(block, block, send.at[n, 3 * (2 - j)], recv.at[n, 3 * (2 - j)], 3 - j).wait_recv()

    def wide(n):
        return pl.ds(pl.multiple_of(n * wide_tile, wide_tile), wide_tile)

    def send_back(n, k):
        return across(
            back_send.at[paired(me, k, owners), :, wide(n)], back_recv.at[me, :, wide(n)],
            back_s.at[n, k], back_r.at[n, k], k,
        )

    def take_back(n, k):
        source = paired(me, k, owners)
        across(
            back_send.at[source, :, wide(n)], back_recv.at[source, :, wide(n)],
            back_s.at[n, k], back_r.at[n, k], k,
        ).wait_recv()

    chip = lax.div(me, 2)
    inner = lax.rem(lax.div(chip + 1, 2), 2)
    out_order, in_order = [1], [1]
    for i in range(3):
        for core in range(2):
            out_order.append(2 * (1 + lax.rem(i + inner, 3)) + core)
            in_order.append(2 * (1 + lax.rem(i + 1 - inner, 3)) + core)
    for k in out_order:
        send_block(send_tok, rows, tok_s, tok_r, k).start()

    @pl.loop(0, width // wide_tile)
    def _(n):
        cols = pl.ds(pl.multiple_of(n * wide_tile, wide_tile), wide_tile)
        picked = jnp.dot(pick[...], cot_ref[:, cols], preferred_element_type=F32)
        picked = picked * gate_col[:, 0:1]
        send_cot[:, :, cols] = picked.astype(BF16).reshape(owners, capacity, wide_tile)

    rows[me] = send_tok[me]
    scaled[me] = send_cot[me]
    for j in range(1, groups):
        share(rows, x_rows, fr_s, fr_r, 0, j).start()
    for out, k in zip(out_order, in_order):
        send_block(send_tok, rows, tok_s, tok_r, out).wait_send()
        send_block(send_cot, scaled, cot_s, cot_r, out).start()
        take_block(send_tok, rows, tok_s, tok_r, k)
        for j in range(1, groups):
            share(rows, x_rows, fr_s, fr_r, k, j).start()

    mine = pl.ds(pl.multiple_of(grp * part, part), part)
    own_rows = pltpu.make_async_copy(rows.at[:, :, mine], x_rows.at[grp], own_sem.at[0])
    own_rows.start()
    weight_copies[0].wait()
    weight_copies[1].wait()

    @pl.loop(0, hid_width // hid_tile)
    def _(n):
        cols = pl.ds(pl.multiple_of(n * hid_tile, hid_tile), hid_tile)
        held = rows[...].reshape(slots, width)
        gate = jnp.dot(held, wg[:, cols], preferred_element_type=F32)
        up = jnp.dot(held, wu[:, cols], preferred_element_type=F32)
        sig = jax.nn.sigmoid(gate)
        active = gate * sig
        x_hid[grp, :, cols] = (active * up).astype(BF16)
        gate_factor[:, cols] = up * sig * (1.0 + gate * (1.0 - sig))
        up_factor[:, cols] = active

    for j in (1, 2):
        spread(x_hid, h_s, h_r, j).start()
    for j in range(1, groups):
        share(scaled, x_scaled, fc_s, fc_r, 0, j).start()
    for step, k in enumerate(in_order):
        take_block(send_cot, scaled, cot_s, cot_r, k)
        for j in range(1, groups):
            share(scaled, x_scaled, fc_s, fc_r, k, j).start()
        if step == owners // 2:
            for j in (1, 2):
                take_spread(x_hid, h_s, h_r, j)
                hand_on(x_hid, h_s, h_r, j).start()
    own_scaled = pltpu.make_async_copy(scaled.at[:, :, mine], x_scaled.at[grp], own_sem.at[1])
    own_scaled.start()
    weight_copies[2].wait()
    score[...] = jnp.zeros_like(score)

    @pl.loop(0, hid_width // hid_tile)
    def _(n):
        cols = pl.ds(pl.multiple_of(n * hid_tile, hid_tile), hid_tile)
        grad_hidden = dot_nt(scaled[...].reshape(slots, width), wd[cols, :])
        x_gg[grp, :, cols] = (grad_hidden * gate_factor[:, cols]).astype(BF16)
        x_gu[grp, :, cols] = (grad_hidden * up_factor[:, cols]).astype(BF16)
        for j in (1, 2):
            spread_tile(x_gg, gg_s, gg_r, n, j).start()
            spread_tile(x_gu, gu_s, gu_r, n, j).start()
        score[...] += jnp.broadcast_to(
            jnp.sum(x_hid[grp, :, cols].astype(F32) * grad_hidden, axis=1, keepdims=True),
            (slots, 128),
        )

    @pl.loop(0, width // wide_tile)
    def _(n):
        cols = pl.ds(pl.multiple_of(n * wide_tile, wide_tile), wide_tile)
        grad = dot_nt(x_gg[grp], wg[cols, :]) + dot_nt(x_gu[grp], wu[cols, :])
        back_send[:, :, cols] = grad.astype(BF16).reshape(owners, capacity, wide_tile)
        for k in out_order:
            send_back(n, k).start()
        back_recv[me, :, cols] = back_send[me, :, cols]

    on_diagonal = lax.broadcasted_iota(jnp.int32, (capacity, 128), 0) == lax.broadcasted_iota(
        jnp.int32, (capacity, 128), 1
    )
    for e in range(owners):
        line = jnp.sum(
            jnp.where(on_diagonal, score[e * capacity:(e + 1) * capacity, :], 0.0),
            axis=0, keepdims=True,
        )
        score_send[e] = jnp.broadcast_to(line, (8, 128))
    for k in out_order:
        send_block(score_send, score_recv, sc_s, sc_r, k).start()
    score_recv[me] = score_send[me]

    own_rows.wait()
    own_scaled.wait()
    for j in (1, 2):
        take_on(x_hid, h_s, h_r, j)
    for j in range(1, groups):
        for k in range(owners):
            take_share(rows, x_rows, fr_s, fr_r, k, j)
            take_share(scaled, x_scaled, fc_s, fc_r, k, j)

    @pl.loop(0, hid_width // hid_tile)
    def _(n):
        cols = pl.ds(pl.multiple_of(n * hid_tile, hid_tile), hid_tile)
        gwd_ref[cols, :] = dot_tn(
            x_hid[:, :, cols].reshape(groups * slots, hid_tile),
            x_scaled[...].reshape(groups * slots, part),
        ).astype(BF16)

    def terms(origin, cols):
        left = x_rows[origin].reshape(slots, part)
        return dot_tn(left, x_gg[origin, :, cols]), dot_tn(left, x_gu[origin, :, cols])

    @pl.loop(0, hid_width // hid_tile)
    def _(n):
        acc_gate[:, tile(n)], acc_up[:, tile(n)] = terms(grp, tile(n))

    @pl.loop(0, hid_width // hid_tile)
    def _(n):
        for j in (1, 2):
            take_tile(x_gg, gg_s, gg_r, n, j)
            hand_on_tile(x_gg, gg_s, gg_r, n, j).start()
            take_tile(x_gu, gu_s, gu_r, n, j)
            hand_on_tile(x_gu, gu_s, gu_r, n, j).start()
        for j in (1, 2):
            gate, up = terms(paired(grp, j, groups), tile(n))
            acc_gate[:, tile(n)] += gate
            acc_up[:, tile(n)] += up

    def combine(n):
        for k in range(1, owners):
            take_back(n, k)
        gtok_ref[:, wide(n)] = dot_tn(
            pick[...], back_recv[:, :, wide(n)].reshape(slots, wide_tile)
        ).astype(BF16)

    def finish(n):
        for j in (1, 2):
            take_on_tile(x_gg, gg_s, gg_r, n, j)
            take_on_tile(x_gu, gu_s, gu_r, n, j)
        gate, up = terms(paired(grp, 3, groups), tile(n))
        gwg_ref[:, tile(n)] = (acc_gate[:, tile(n)] + gate).astype(BF16)
        gwu_ref[:, tile(n)] = (acc_up[:, tile(n)] + up).astype(BF16)

    pl.loop(0, width // wide_tile - 1)(combine)
    pl.loop(0, hid_width // hid_tile - 1)(finish)
    combine(width // wide_tile - 1)

    for k in range(1, owners):
        take_block(score_send, score_recv, sc_s, sc_r, k)
    first_sum = jnp.zeros((1, tok_count), F32)
    second_sum = jnp.zeros((1, tok_count), F32)
    for e in range(owners):
        column = jnp.sum(
            jnp.where(on_diagonal, jnp.broadcast_to(score_recv[e, 0:1, :], (capacity, 128)), 0.0),
            axis=1, keepdims=True,
        )
        by_token = jnp.sum(
            pick[e * capacity:(e + 1) * capacity, :].astype(F32) * column, axis=0, keepdims=True
        )
        first_sum = first_sum + jnp.where(ids_ref[0:1, :] == e, by_token, 0.0)
        second_sum = second_sum + jnp.where(ids_ref[1:2, :] == e, by_token, 0.0)
    weights = gates_ref[...].astype(F32)
    ggate_ref[...] = (jnp.concatenate([first_sum, second_sum], axis=0) / weights).astype(BF16)

    finish(hid_width // hid_tile - 1)

    for k in range(1, owners):
        send_block(send_cot, scaled, cot_s, cot_r, k).wait_send()
        send_block(score_send, score_recv, sc_s, sc_r, k).wait_send()
    @pl.loop(0, width // wide_tile)
    def _(n):
        for k in range(1, owners):
            send_back(n, k).wait_send()

    @pl.loop(0, hid_width // hid_tile)
    def _(n):
        for j in (1, 2):
            for held, send, recv in ((x_gg, gg_s, gg_r), (x_gu, gu_s, gu_r)):
                spread_tile(held, send, recv, n, j).wait_send()
                hand_on_tile(held, send, recv, n, j).wait_send()

    for j in (1, 2):
        spread(x_hid, h_s, h_r, j).wait_send()
        hand_on(x_hid, h_s, h_r, j).wait_send()
    for j in range(1, groups):
        for k in range(owners):
            share(rows, x_rows, fr_s, fr_r, k, j).wait_send()
            share(scaled, x_scaled, fc_s, fc_r, k, j).wait_send()


def hand_over(*refs):
    count = len(refs) // 2
    for i in range(count):
        refs[count + i][...] = refs[i][...]


def kernel_body(tokens, expert_ids, gates, cotangent, w_gate, w_up, w_down):
    tok_rows, width = tokens.shape
    owners = lax.axis_size("expert")
    groups = lax.axis_size("dp")
    capacity = slots_of(tok_rows, expert_ids.shape[1], owners)
    hid_width = w_gate.shape[2]
    part = width // groups
    slots = owners * capacity
    vmem = pl.BlockSpec(memory_space=pltpu.VMEM)
    dma = pltpu.SemaphoreType.DMA
    blocks = pltpu.VMEM((owners, capacity, width), BF16)
    parts = pltpu.VMEM((groups, owners, capacity, part), BF16)
    hids = pltpu.VMEM((groups, slots, hid_width), BF16)
    lines = pltpu.VMEM((owners, 8, 128), F32)
    per_back = dma((width // tile_of(width, 512), owners))
    per_tile = dma((hid_width // tile_of(hid_width, 256), groups))
    per_owner, per_group, per_share = dma((owners,)), dma((groups,)), dma((owners, groups))
    grad_tokens, grad_gates, grad_gate, grad_up, grad_down = pl.pallas_call(
        functools.partial(layer_kernel, owners, groups, capacity),
        out_shape=(
            jax.ShapeDtypeStruct((tok_rows, width), BF16),
            jax.ShapeDtypeStruct((2, tok_rows), BF16),
            jax.ShapeDtypeStruct((part, hid_width), BF16),
            jax.ShapeDtypeStruct((part, hid_width), BF16),
            jax.ShapeDtypeStruct((hid_width, part), BF16),
        ),
        in_specs=[vmem] * 4 + [pl.BlockSpec(memory_space=pl.ANY)] * 3,
        out_specs=(vmem,) * 5,
        scratch_shapes=[
            pltpu.VMEM((width, hid_width), BF16),
            pltpu.VMEM((width, hid_width), BF16),
            pltpu.VMEM((hid_width, width), BF16),
            dma((3,)),
            pltpu.VMEM((slots, tok_rows), BF16),
            pltpu.VMEM((slots, 128), F32),
            blocks, blocks, blocks, blocks,
            pltpu.VMEM((slots, hid_width), F32),
            pltpu.VMEM((slots, hid_width), F32),
            pltpu.VMEM((slots, 128), F32),
            parts, parts, hids, hids, hids,
            dma((2,)),
            blocks, blocks, lines, lines,
            pltpu.VMEM((part, hid_width), F32),
            pltpu.VMEM((part, hid_width), F32),
        ]
        + [per_owner] * 4 + [per_back] * 2 + [per_owner] * 2 + [per_share] * 4
        + [per_group] * 2 + [per_tile] * 4,
        compiler_params=pltpu.CompilerParams(
            collective_id=0, has_side_effects=True, vmem_limit_bytes=56 * 1024 * 1024
        ),
        cost_estimate=pl.CostEstimate(
            flops=16 * slots * width * hid_width,
            bytes_accessed=6 * width * hid_width * 2,
            transcendentals=2 * slots * hid_width,
        ),
        name="expert_layer",
    )(
        expert_ids.T, gates.T, tokens, cotangent, w_gate, w_up, w_down
    )
    held = (grad_tokens, grad_gates, grad_gate[None], grad_up[None], grad_down[None])
    quarters = [
        pl.BlockSpec(x.shape, lambda n: (0, 0)) if x.shape[0] == 2 else pl.BlockSpec(
            x.shape[:-2] + (x.shape[-2] // 4, x.shape[-1]),
            (lambda n: (n, 0)) if x.ndim == 2 else (lambda n: (0, n, 0)),
        )
        for x in held
    ]
    grad_tokens, grad_gates, grad_gate, grad_up, grad_down = pl.pallas_call(
        hand_over,
        grid=(4,),
        out_shape=tuple(jax.ShapeDtypeStruct(x.shape, x.dtype) for x in held),
        in_specs=quarters,
        out_specs=tuple(quarters),
        name="hand_over",
    )(*held)
    return (grad_tokens, grad_gates.T, grad_gate, grad_up, grad_down)


def contract_rows(left, right):
    return lax.dot_general(
        left, right, (((0,), (0,)), ((), ())), preferred_element_type=jnp.float32
    )


def expert_pass(rows, cot_rows, gate_column, gate_mat, up_mat, down_mat):
    pre_gate = jnp.dot(rows, gate_mat, preferred_element_type=jnp.float32)
    pre_up = jnp.dot(rows, up_mat, preferred_element_type=jnp.float32)
    sigmoid_gate = jax.nn.sigmoid(pre_gate)
    activated = pre_gate * sigmoid_gate
    hidden = (activated * pre_up).astype(jnp.bfloat16)
    expert_out = jnp.dot(hidden, down_mat, preferred_element_type=jnp.float32)
    cot_float = cot_rows.astype(jnp.float32)
    score_grad = jnp.sum(expert_out * cot_float, axis=1)
    scaled = (gate_column.astype(jnp.float32)[:, None] * cot_float).astype(jnp.bfloat16)
    grad_hidden = jnp.dot(scaled, down_mat.T, preferred_element_type=jnp.float32)
    grad_pre_gate = (
        grad_hidden * pre_up * sigmoid_gate * (1.0 + pre_gate * (1.0 - sigmoid_gate))
    ).astype(jnp.bfloat16)
    grad_pre_up = (grad_hidden * activated).astype(jnp.bfloat16)
    row_grad = (
        jnp.dot(grad_pre_gate, gate_mat.T, preferred_element_type=jnp.float32)
        + jnp.dot(grad_pre_up, up_mat.T, preferred_element_type=jnp.float32)
    ).astype(jnp.bfloat16)
    return (hidden, scaled, grad_pre_gate, grad_pre_up, row_grad, score_grad)


def by_owner(values, owners, capacity):
    return values.reshape((owners, capacity) + values.shape[1:])


def sum_weights(part_gate, part_up, part_down):
    return (
        lax.psum_scatter(
            part_gate.astype(jnp.bfloat16), "dp", scatter_dimension=0, tiled=True
        ).astype(jnp.float32),
        lax.psum_scatter(
            part_up.astype(jnp.bfloat16), "dp", scatter_dimension=0, tiled=True
        ).astype(jnp.float32),
        lax.psum_scatter(
            part_down.astype(jnp.bfloat16), "dp", scatter_dimension=1, tiled=True
        ).astype(jnp.float32),
    )


def send_back(row_grad, score_grad, owners, capacity):
    score_half = score_grad.astype(jnp.bfloat16)
    back_rows = lax.all_to_all(
        by_owner(row_grad, owners, capacity), "expert", split_axis=0, concat_axis=0, tiled=True
    )
    back_scores = lax.all_to_all(
        by_owner(score_half, owners, capacity), "expert", split_axis=0, concat_axis=0, tiled=True
    )
    return (back_rows, back_scores)


def plain_body(tokens, expert_ids, gates, cotangent, w_gate, w_up, w_down):
    tok_rows, model_width = tokens.shape
    top_count = expert_ids.shape[1]
    owners = lax.axis_size("expert")
    capacity = min(tok_rows, 3 * tok_rows * top_count // (2 * owners))
    slot_count = owners * capacity
    flat_ids = expert_ids.reshape(-1)
    pair_count = flat_ids.shape[0]
    picked = (flat_ids[:, None] == jnp.arange(owners, dtype=jnp.int32)[None, :]).astype(jnp.int32)
    before = jnp.cumsum(picked, axis=0) - picked
    position = jnp.sum(before * picked, axis=1)
    target = flat_ids * capacity + position
    source_row = jnp.arange(pair_count, dtype=jnp.int32) // top_count
    send_rows = (
        jnp.zeros((slot_count, model_width), jnp.bfloat16).at[target].set(tokens[source_row])
    )
    send_cot = (
        jnp.zeros((slot_count, model_width), jnp.bfloat16).at[target].set(cotangent[source_row])
    )
    send_gate = jnp.zeros((slot_count,), jnp.bfloat16).at[target].set(gates.reshape(-1))
    recv_gate = lax.all_to_all(
        by_owner(send_gate, owners, capacity), "expert", split_axis=0, concat_axis=0, tiled=True
    )
    recv_rows = lax.all_to_all(
        by_owner(send_rows, owners, capacity), "expert", split_axis=0, concat_axis=0, tiled=True
    )
    recv_cot = lax.all_to_all(
        by_owner(send_cot, owners, capacity), "expert", split_axis=0, concat_axis=0, tiled=True
    )
    rows = recv_rows.reshape(slot_count, model_width)
    cot_rows = recv_cot.reshape(slot_count, model_width)
    gate_column = recv_gate.reshape(slot_count)
    hidden, scaled, grad_pre_gate, grad_pre_up, row_grad, score_grad = expert_pass(
        rows, cot_rows, gate_column, w_gate[0], w_up[0], w_down[0]
    )
    part_gate = contract_rows(rows, grad_pre_gate)
    part_up = contract_rows(rows, grad_pre_up)
    part_down = contract_rows(hidden, scaled)
    back_rows, back_scores = send_back(row_grad, score_grad, owners, capacity)
    summed = sum_weights(part_gate, part_up, part_down)
    pair_rows = back_rows.reshape(slot_count, model_width)[target].reshape(
        tok_rows, top_count, model_width
    )
    grad_tokens = jnp.sum(pair_rows.astype(jnp.float32), axis=1).astype(jnp.bfloat16)
    grad_gates = back_scores.reshape(slot_count)[target].reshape(tok_rows, top_count)
    grad_w_gate = summed[0].astype(jnp.bfloat16)[None]
    grad_w_up = summed[1].astype(jnp.bfloat16)[None]
    grad_w_down = summed[2].astype(jnp.bfloat16)[None]
    return (grad_tokens, grad_gates, grad_w_gate, grad_w_up, grad_w_down)


def slots_of(tok_rows, top_count, owners):
    return min(tok_rows, 3 * tok_rows * top_count // (2 * owners))


def body(tokens, expert_ids, gates, cotangent, w_gate, w_up, w_down):
    capacity = slots_of(tokens.shape[0], expert_ids.shape[1], lax.axis_size("expert"))
    even = lax.axis_size("dp") == 4 and lax.axis_size("expert") == 8
    chosen = kernel_body if even and capacity % 16 == 0 else plain_body
    return chosen(tokens, expert_ids, gates, cotangent, w_gate, w_up, w_down)


def solution(mesh):
    placed = (
        P(("dp", "expert"), None),
        P(("dp", "expert"), None),
        P(("dp", "expert"), None),
        P(("dp", "expert"), None),
        P("expert", None, None),
        P("expert", None, None),
        P("expert", None, None),
    )
    return jax.shard_map(
        body,
        mesh=mesh,
        in_specs=placed,
        out_specs=(
            P(("dp", "expert"), None),
            P(("dp", "expert"), None),
            P("expert", "dp", None),
            P("expert", "dp", None),
            P("expert", None, "dp"),
        ),
        check_vma=False,
    )
```

```python
import functools

import jax
import jax.numpy as jnp
from jax import lax
from jax.experimental import pallas as pl
from jax.experimental.pallas import tpu as pltpu
from jax.sharding import PartitionSpec as P

MESH = pl.DeviceIdType.MESH
F32 = jnp.float32
BF16 = jnp.bfloat16


def tile_of(size, most):
    step = min(size, most)
    while size % step:
        step -= 128
    return step


def paired(index, step, count):
    total, digit = 0, 1
    while digit < count:
        total = total + digit * lax.rem(lax.div(index, digit) + lax.div(step, digit), 2)
        digit *= 2
    return total


def dot_nt(left, right):
    return lax.dot_general(left, right, (((1,), (1,)), ((), ())), preferred_element_type=F32)


def dot_tn(left, right):
    return lax.dot_general(left, right, (((0,), (0,)), ((), ())), preferred_element_type=F32)


def layer_kernel(
    owners, groups, capacity,
    ids_ref, gates_ref, tok_ref, cot_ref, wg_hbm, wu_hbm, wd_hbm,
    gtok_ref, ggate_ref, gwg_ref, gwu_ref, gwd_ref,
    wg, wu, wd, w_sem,
    pick, gate_col, send_tok, send_cot, rows, scaled, gate_factor, up_factor, score,
    x_rows, x_scaled, x_hid, x_gg, x_gu, own_sem,
    back_send, back_recv, score_send, score_recv, acc_gate, acc_up,
    tok_s, tok_r, cot_s, cot_r, back_s, back_r, sc_s, sc_r,
    fr_s, fr_r, fc_s, fc_r, h_s, h_r, gg_s, gg_r, gu_s, gu_r,
):
    me = lax.axis_index("expert")
    grp = lax.axis_index("dp")
    tok_count, width = tok_ref.shape
    slots = owners * capacity
    hid_width = wg.shape[1]
    part = width // groups
    hid_tile = tile_of(hid_width, 256)
    wide_tile = tile_of(width, 512)

    weight_copies = [
        pltpu.make_async_copy(src.at[0], dst, w_sem.at[i])
        for i, (src, dst) in enumerate(((wg_hbm, wg), (wu_hbm, wu), (wd_hbm, wd)))
    ]
    for copy in weight_copies:
        copy.start()

    barrier = pltpu.get_barrier_semaphore()
    for k in range(1, owners):
        pl.semaphore_signal(
            barrier, inc=1, device_id={"expert": paired(me, k, owners)}, device_id_type=MESH
        )
    for j in range(1, groups):
        pl.semaphore_signal(
            barrier, inc=1, device_id={"dp": paired(grp, j, groups)}, device_id_type=MESH
        )

    expert_no = lax.broadcasted_iota(jnp.int32, (owners, tok_count), 0)
    first = ids_ref[0:1, :] == expert_no
    second = ids_ref[1:2, :] == expert_no
    named = jnp.where(first, 1.0, 0.0) + jnp.where(second, 1.0, 0.0)
    weights = gates_ref[...].astype(F32)
    gate_of = jnp.where(first, weights[0:1, :], 0.0) + jnp.where(second, weights[1:2, :], 0.0)
    earlier = jnp.where(
        lax.broadcasted_iota(jnp.int32, (tok_count, tok_count), 0)
        < lax.broadcasted_iota(jnp.int32, (tok_count, tok_count), 1),
        1.0, 0.0,
    ).astype(BF16)
    position = jnp.dot(named.astype(BF16), earlier, preferred_element_type=F32)
    position = jnp.where(named > 0.5, position, -1.0)
    slot_no = lax.broadcasted_iota(jnp.int32, (capacity, tok_count), 0).astype(F32)
    for e in range(owners):
        chosen = jnp.where(slot_no == position[e:e + 1, :], 1.0, 0.0)
        pick[e * capacity:(e + 1) * capacity, :] = chosen.astype(BF16)
        gate_col[e * capacity:(e + 1) * capacity, :] = jnp.broadcast_to(
            jnp.sum(chosen * gate_of[e:e + 1, :], axis=1, keepdims=True), (capacity, 128)
        )

    @pl.loop(0, width // wide_tile)
    def _(n):
        cols = pl.ds(pl.multiple_of(n * wide_tile, wide_tile), wide_tile)
        picked = jnp.dot(pick[...], tok_ref[:, cols], preferred_element_type=F32)
        send_tok[:, :, cols] = picked.astype(BF16).reshape(owners, capacity, wide_tile)

    pl.semaphore_wait(barrier, owners - 1 + groups - 1)

    def across(src, dst, send, recv, k):
        return pltpu.make_async_remote_copy(
            src_ref=src, dst_ref=dst, send_sem=send, recv_sem=recv,
            device_id={"expert": paired(me, k, owners)}, device_id_type=MESH,
        )

    def aside(src, dst, send, recv, j):
        return pltpu.make_async_remote_copy(
            src_ref=src, dst_ref=dst, send_sem=send, recv_sem=recv,
            device_id={"dp": paired(grp, j, groups)}, device_id_type=MESH,
        )

    def send_block(sent, held, send, recv, k):
        return across(sent.at[paired(me, k, owners)], held.at[me], send.at[k], recv.at[k], k)

    def take_block(sent, held, send, recv, k):
        source = paired(me, k, owners)
        across(sent.at[source], held.at[source], send.at[k], recv.at[k], k).wait_recv()
        return source

    def share(held, parts, send, recv, k, j):
        source = paired(me, k, owners)
        target = paired(grp, j, groups)
        cols = pl.ds(pl.multiple_of(target * part, part), part)
        return aside(
            held.at[source, :, cols], parts.at[grp, source], send.at[k, j], recv.at[k, j], j
        )

    def take_share(held, parts, send, recv, k, j):
        source = paired(me, k, owners)
        origin = paired(grp, j, groups)
        aside(
            held.at[source, :, pl.ds(0, part)], parts.at[origin, source],
            send.at[k, j], recv.at[k, j], j,
        ).wait_recv()

    def spread(held, send, recv, j):
        return aside(held.at[grp], held.at[grp], send.at[j], recv.at[j], j)

    def take_spread(held, send, recv, j):
        origin = paired(grp, j, groups)
        aside(held.at[origin], held.at[origin], send.at[j], recv.at[j], j).wait_recv()
        return origin

    def hand_on(held, send, recv, j):
        half = slots // 2
        source = paired(grp, j, groups)
        lines = pl.ds((j - 1) * half, half)
        block = held.at[source, lines]
        return aside(block, block, send.at[3 * (2 - j)], recv.at[3 * (2 - j)], 3 - j)

    def take_on(held, send, recv, j):
        half = slots // 2
        block = held.at[paired(grp, 3, groups), pl.ds((j - 1) * half, half)]
        aside(block, block, send.at[3 * (2 - j)], recv.at[3 * (2 - j)], 3 - j).wait_recv()

    def tile(n):
        return pl.ds(pl.multiple_of(n * hid_tile, hid_tile), hid_tile)

    def spread_tile(held, send, recv, n, j):
        block = held.at[grp, :, tile(n)]
        return aside(block, block, send.at[n, j], recv.at[n, j], j)

    def take_tile(held, send, recv, n, j):
        block = held.at[paired(grp, j, groups), :, tile(n)]
        aside(block, block, send.at[n, j], recv.at[n, j], j).wait_recv()

    def hand_on_tile(held, send, recv, n, j):
        half = slots // 2
        block = held.at[paired(grp, j, groups), pl.ds((j - 1) * half, half), tile(n)]
        return aside(block, block, send.at[n, 3 * (2 - j)], recv.at[n, 3 * (2 - j)], 3 - j)

    def take_on_tile(held, send, recv, n, j):
        half = slots // 2
        block = held.at[paired(grp, 3, groups), pl.ds((j - 1) * half, half), tile(n)]
        aside(block, block, send.at[n, 3 * (2 - j)], recv.at[n, 3 * (2 - j)], 3 - j).wait_recv()

    def wide(n):
        return pl.ds(pl.multiple_of(n * wide_tile, wide_tile), wide_tile)

    def send_back(n, k):
        return across(
            back_send.at[paired(me, k, owners), :, wide(n)], back_recv.at[me, :, wide(n)],
            back_s.at[n, k], back_r.at[n, k], k,
        )

    def take_back(n, k):
        source = paired(me, k, owners)
        across(
            back_send.at[source, :, wide(n)], back_recv.at[source, :, wide(n)],
            back_s.at[n, k], back_r.at[n, k], k,
        ).wait_recv()

    chip = lax.div(me, 2)
    turn = lax.rem(me, 2)
    near = (1 + turn, 2 - turn)
    aside_order = near + (3,)
    inner = lax.rem(lax.div(chip + 1, 2), 2)
    out_order, in_order = [1], [1]
    for i in range(3):
        for core in range(2):
            out_order.append(2 * (1 + lax.rem(i + inner, 3)) + core)
            in_order.append(2 * (1 + lax.rem(i + 1 - inner, 3)) + core)
    for k in out_order:
        send_block(send_tok, rows, tok_s, tok_r, k).start()

    @pl.loop(0, width // wide_tile)
    def _(n):
        cols = pl.ds(pl.multiple_of(n * wide_tile, wide_tile), wide_tile)
        picked = jnp.dot(pick[...], cot_ref[:, cols], preferred_element_type=F32)
        picked = picked * gate_col[:, 0:1]
        send_cot[:, :, cols] = picked.astype(BF16).reshape(owners, capacity, wide_tile)

    rows[me] = send_tok[me]
    scaled[me] = send_cot[me]
    for j in aside_order:
        share(rows, x_rows, fr_s, fr_r, 0, j).start()
    for out, k in zip(out_order, in_order):
        send_block(send_tok, rows, tok_s, tok_r, out).wait_send()
        send_block(send_cot, scaled, cot_s, cot_r, out).start()
        take_block(send_tok, rows, tok_s, tok_r, k)
        for j in aside_order:
            share(rows, x_rows, fr_s, fr_r, k, j).start()

    mine = pl.ds(pl.multiple_of(grp * part, part), part)
    own_rows = pltpu.make_async_copy(rows.at[:, :, mine], x_rows.at[grp], own_sem.at[0])
    own_rows.start()
    weight_copies[0].wait()
    weight_copies[1].wait()

    @pl.loop(0, hid_width // hid_tile)
    def _(n):
        cols = pl.ds(pl.multiple_of(n * hid_tile, hid_tile), hid_tile)
        held = rows[...].reshape(slots, width)
        gate = jnp.dot(held, wg[:, cols], preferred_element_type=F32)
        up = jnp.dot(held, wu[:, cols], preferred_element_type=F32)
        sig = jax.nn.sigmoid(gate)
        active = gate * sig
        x_hid[grp, :, cols] = (active * up).astype(BF16)
        gate_factor[:, cols] = up * sig * (1.0 + gate * (1.0 - sig))
        up_factor[:, cols] = active

    for j in near:
        spread(x_hid, h_s, h_r, j).start()
    for j in aside_order:
        share(scaled, x_scaled, fc_s, fc_r, 0, j).start()
    for step, k in enumerate(in_order):
        take_block(send_cot, scaled, cot_s, cot_r, k)
        for j in aside_order:
            share(scaled, x_scaled, fc_s, fc_r, k, j).start()
        if step == owners // 2:
            for j in near:
                take_spread(x_hid, h_s, h_r, j)
                hand_on(x_hid, h_s, h_r, j).start()
    own_scaled = pltpu.make_async_copy(scaled.at[:, :, mine], x_scaled.at[grp], own_sem.at[1])
    own_scaled.start()
    weight_copies[2].wait()
    score[...] = jnp.zeros_like(score)

    @pl.loop(0, hid_width // hid_tile)
    def _(n):
        cols = pl.ds(pl.multiple_of(n * hid_tile, hid_tile), hid_tile)
        grad_hidden = dot_nt(scaled[...].reshape(slots, width), wd[cols, :])
        x_gg[grp, :, cols] = (grad_hidden * gate_factor[:, cols]).astype(BF16)
        x_gu[grp, :, cols] = (grad_hidden * up_factor[:, cols]).astype(BF16)
        for j in near:
            spread_tile(x_gg, gg_s, gg_r, n, j).start()
            spread_tile(x_gu, gu_s, gu_r, n, j).start()
        score[...] += jnp.broadcast_to(
            jnp.sum(x_hid[grp, :, cols].astype(F32) * grad_hidden, axis=1, keepdims=True),
            (slots, 128),
        )

    def go_back(n):
        cols = wide(n)
        grad = dot_nt(x_gg[grp], wg[cols, :]) + dot_nt(x_gu[grp], wu[cols, :])
        back_send[:, :, cols] = grad.astype(BF16).reshape(owners, capacity, wide_tile)
        back_recv[me, :, cols] = back_send[me, :, cols]

    def start_back(n):
        for k in out_order:
            send_back(n, k).start()

    wide_tiles, hid_tiles = width // wide_tile, hid_width // hid_tile

    @pl.loop(0, wide_tiles // 2)
    def _(n):
        go_back(n)
        start_back(n)

    pl.loop(wide_tiles // 2, wide_tiles)(go_back)

    on_diagonal = lax.broadcasted_iota(jnp.int32, (capacity, 128), 0) == lax.broadcasted_iota(
        jnp.int32, (capacity, 128), 1
    )
    for e in range(owners):
        line = jnp.sum(
            jnp.where(on_diagonal, score[e * capacity:(e + 1) * capacity, :], 0.0),
            axis=0, keepdims=True,
        )
        score_send[e] = jnp.broadcast_to(line, (8, 128))
    for k in out_order:
        send_block(score_send, score_recv, sc_s, sc_r, k).start()
    score_recv[me] = score_send[me]

    own_rows.wait()
    own_scaled.wait()
    for j in (1, 2):
        take_on(x_hid, h_s, h_r, j)
    for j in range(1, groups):
        for k in range(owners):
            take_share(rows, x_rows, fr_s, fr_r, k, j)
            take_share(scaled, x_scaled, fc_s, fc_r, k, j)

    @pl.loop(0, hid_width // hid_tile)
    def _(n):
        cols = pl.ds(pl.multiple_of(n * hid_tile, hid_tile), hid_tile)
        gwd_ref[cols, :] = dot_tn(
            x_hid[:, :, cols].reshape(groups * slots, hid_tile),
            x_scaled[...].reshape(groups * slots, part),
        ).astype(BF16)

    def terms(origin, cols):
        left = x_rows[origin].reshape(slots, part)
        return dot_tn(left, x_gg[origin, :, cols]), dot_tn(left, x_gu[origin, :, cols])

    @pl.loop(0, hid_width // hid_tile)
    def _(n):
        acc_gate[:, tile(n)], acc_up[:, tile(n)] = terms(grp, tile(n))

    @pl.loop(0, hid_tiles)
    def _(n):
        for j in near:
            take_tile(x_gg, gg_s, gg_r, n, j)
            hand_on_tile(x_gg, gg_s, gg_r, n, j).start()
            take_tile(x_gu, gu_s, gu_r, n, j)
            hand_on_tile(x_gu, gu_s, gu_r, n, j).start()
        later = wide_tiles - wide_tiles // 2

        @pl.loop(wide_tiles // 2 + (n * later + hid_tiles - 1) // hid_tiles,
                 wide_tiles // 2 + ((n + 1) * later + hid_tiles - 1) // hid_tiles)
        def _(m):
            start_back(m)

        for j in (1, 2):
            gate, up = terms(paired(grp, j, groups), tile(n))
            acc_gate[:, tile(n)] += gate
            acc_up[:, tile(n)] += up

    def combine(n):
        for k in range(1, owners):
            take_back(n, k)
        gtok_ref[:, wide(n)] = dot_tn(
            pick[...], back_recv[:, :, wide(n)].reshape(slots, wide_tile)
        ).astype(BF16)

    def finish(n):
        for j in (1, 2):
            take_on_tile(x_gg, gg_s, gg_r, n, j)
            take_on_tile(x_gu, gu_s, gu_r, n, j)
        gate, up = terms(paired(grp, 3, groups), tile(n))
        gwg_ref[:, tile(n)] = (acc_gate[:, tile(n)] + gate).astype(BF16)
        gwu_ref[:, tile(n)] = (acc_up[:, tile(n)] + up).astype(BF16)

    pl.loop(0, width // wide_tile - 1)(combine)
    pl.loop(0, hid_width // hid_tile - 1)(finish)
    combine(width // wide_tile - 1)

    for k in range(1, owners):
        take_block(score_send, score_recv, sc_s, sc_r, k)
    first_sum = jnp.zeros((1, tok_count), F32)
    second_sum = jnp.zeros((1, tok_count), F32)
    for e in range(owners):
        column = jnp.sum(
            jnp.where(on_diagonal, jnp.broadcast_to(score_recv[e, 0:1, :], (capacity, 128)), 0.0),
            axis=1, keepdims=True,
        )
        by_token = jnp.sum(
            pick[e * capacity:(e + 1) * capacity, :].astype(F32) * column, axis=0, keepdims=True
        )
        first_sum = first_sum + jnp.where(ids_ref[0:1, :] == e, by_token, 0.0)
        second_sum = second_sum + jnp.where(ids_ref[1:2, :] == e, by_token, 0.0)
    weights = gates_ref[...].astype(F32)
    ggate_ref[...] = (jnp.concatenate([first_sum, second_sum], axis=0) / weights).astype(BF16)

    finish(hid_width // hid_tile - 1)

    for k in range(1, owners):
        send_block(send_cot, scaled, cot_s, cot_r, k).wait_send()
        send_block(score_send, score_recv, sc_s, sc_r, k).wait_send()
    @pl.loop(0, width // wide_tile)
    def _(n):
        for k in range(1, owners):
            send_back(n, k).wait_send()

    @pl.loop(0, hid_width // hid_tile)
    def _(n):
        for j in (1, 2):
            for held, send, recv in ((x_gg, gg_s, gg_r), (x_gu, gu_s, gu_r)):
                spread_tile(held, send, recv, n, j).wait_send()
                hand_on_tile(held, send, recv, n, j).wait_send()

    for j in (1, 2):
        spread(x_hid, h_s, h_r, j).wait_send()
        hand_on(x_hid, h_s, h_r, j).wait_send()
    for j in range(1, groups):
        for k in range(owners):
            share(rows, x_rows, fr_s, fr_r, k, j).wait_send()
            share(scaled, x_scaled, fc_s, fc_r, k, j).wait_send()


def hand_over(*refs):
    count = len(refs) // 2
    for i in range(count):
        refs[count + i][...] = refs[i][...]


def kernel_body(tokens, expert_ids, gates, cotangent, w_gate, w_up, w_down):
    tok_rows, width = tokens.shape
    owners = lax.axis_size("expert")
    groups = lax.axis_size("dp")
    capacity = slots_of(tok_rows, expert_ids.shape[1], owners)
    hid_width = w_gate.shape[2]
    part = width // groups
    slots = owners * capacity
    vmem = pl.BlockSpec(memory_space=pltpu.VMEM)
    dma = pltpu.SemaphoreType.DMA
    blocks = pltpu.VMEM((owners, capacity, width), BF16)
    parts = pltpu.VMEM((groups, owners, capacity, part), BF16)
    hids = pltpu.VMEM((groups, slots, hid_width), BF16)
    lines = pltpu.VMEM((owners, 8, 128), F32)
    per_back = dma((width // tile_of(width, 512), owners))
    per_tile = dma((hid_width // tile_of(hid_width, 256), groups))
    per_owner, per_group, per_share = dma((owners,)), dma((groups,)), dma((owners, groups))
    grad_tokens, grad_gates, grad_gate, grad_up, grad_down = pl.pallas_call(
        functools.partial(layer_kernel, owners, groups, capacity),
        out_shape=(
            jax.ShapeDtypeStruct((tok_rows, width), BF16),
            jax.ShapeDtypeStruct((2, tok_rows), BF16),
            jax.ShapeDtypeStruct((part, hid_width), BF16),
            jax.ShapeDtypeStruct((part, hid_width), BF16),
            jax.ShapeDtypeStruct((hid_width, part), BF16),
        ),
        in_specs=[vmem] * 4 + [pl.BlockSpec(memory_space=pl.ANY)] * 3,
        out_specs=(vmem,) * 5,
        scratch_shapes=[
            pltpu.VMEM((width, hid_width), BF16),
            pltpu.VMEM((width, hid_width), BF16),
            pltpu.VMEM((hid_width, width), BF16),
            dma((3,)),
            pltpu.VMEM((slots, tok_rows), BF16),
            pltpu.VMEM((slots, 128), F32),
            blocks, blocks, blocks, blocks,
            pltpu.VMEM((slots, hid_width), F32),
            pltpu.VMEM((slots, hid_width), F32),
            pltpu.VMEM((slots, 128), F32),
            parts, parts, hids, hids, hids,
            dma((2,)),
            blocks, blocks, lines, lines,
            pltpu.VMEM((part, hid_width), F32),
            pltpu.VMEM((part, hid_width), F32),
        ]
        + [per_owner] * 4 + [per_back] * 2 + [per_owner] * 2 + [per_share] * 4
        + [per_group] * 2 + [per_tile] * 4,
        compiler_params=pltpu.CompilerParams(
            collective_id=0, has_side_effects=True, vmem_limit_bytes=56 * 1024 * 1024
        ),
        cost_estimate=pl.CostEstimate(
            flops=16 * slots * width * hid_width,
            bytes_accessed=6 * width * hid_width * 2,
            transcendentals=2 * slots * hid_width,
        ),
        name="expert_layer",
    )(
        expert_ids.T, gates.T, tokens, cotangent, w_gate, w_up, w_down
    )
    held = (grad_tokens, grad_gates, grad_gate[None], grad_up[None], grad_down[None])
    quarters = [
        pl.BlockSpec(x.shape, lambda n: (0, 0)) if x.shape[0] == 2 else pl.BlockSpec(
            x.shape[:-2] + (x.shape[-2] // 4, x.shape[-1]),
            (lambda n: (n, 0)) if x.ndim == 2 else (lambda n: (0, n, 0)),
        )
        for x in held
    ]
    grad_tokens, grad_gates, grad_gate, grad_up, grad_down = pl.pallas_call(
        hand_over,
        grid=(4,),
        out_shape=tuple(jax.ShapeDtypeStruct(x.shape, x.dtype) for x in held),
        in_specs=quarters,
        out_specs=tuple(quarters),
        name="hand_over",
    )(*held)
    return (grad_tokens, grad_gates.T, grad_gate, grad_up, grad_down)


def contract_rows(left, right):
    return lax.dot_general(
        left, right, (((0,), (0,)), ((), ())), preferred_element_type=jnp.float32
    )


def expert_pass(rows, cot_rows, gate_column, gate_mat, up_mat, down_mat):
    pre_gate = jnp.dot(rows, gate_mat, preferred_element_type=jnp.float32)
    pre_up = jnp.dot(rows, up_mat, preferred_element_type=jnp.float32)
    sigmoid_gate = jax.nn.sigmoid(pre_gate)
    activated = pre_gate * sigmoid_gate
    hidden = (activated * pre_up).astype(jnp.bfloat16)
    expert_out = jnp.dot(hidden, down_mat, preferred_element_type=jnp.float32)
    cot_float = cot_rows.astype(jnp.float32)
    score_grad = jnp.sum(expert_out * cot_float, axis=1)
    scaled = (gate_column.astype(jnp.float32)[:, None] * cot_float).astype(jnp.bfloat16)
    grad_hidden = jnp.dot(scaled, down_mat.T, preferred_element_type=jnp.float32)
    grad_pre_gate = (
        grad_hidden * pre_up * sigmoid_gate * (1.0 + pre_gate * (1.0 - sigmoid_gate))
    ).astype(jnp.bfloat16)
    grad_pre_up = (grad_hidden * activated).astype(jnp.bfloat16)
    row_grad = (
        jnp.dot(grad_pre_gate, gate_mat.T, preferred_element_type=jnp.float32)
        + jnp.dot(grad_pre_up, up_mat.T, preferred_element_type=jnp.float32)
    ).astype(jnp.bfloat16)
    return (hidden, scaled, grad_pre_gate, grad_pre_up, row_grad, score_grad)


def by_owner(values, owners, capacity):
    return values.reshape((owners, capacity) + values.shape[1:])


def sum_weights(part_gate, part_up, part_down):
    return (
        lax.psum_scatter(
            part_gate.astype(jnp.bfloat16), "dp", scatter_dimension=0, tiled=True
        ).astype(jnp.float32),
        lax.psum_scatter(
            part_up.astype(jnp.bfloat16), "dp", scatter_dimension=0, tiled=True
        ).astype(jnp.float32),
        lax.psum_scatter(
            part_down.astype(jnp.bfloat16), "dp", scatter_dimension=1, tiled=True
        ).astype(jnp.float32),
    )


def send_back(row_grad, score_grad, owners, capacity):
    score_half = score_grad.astype(jnp.bfloat16)
    back_rows = lax.all_to_all(
        by_owner(row_grad, owners, capacity), "expert", split_axis=0, concat_axis=0, tiled=True
    )
    back_scores = lax.all_to_all(
        by_owner(score_half, owners, capacity), "expert", split_axis=0, concat_axis=0, tiled=True
    )
    return (back_rows, back_scores)


def plain_body(tokens, expert_ids, gates, cotangent, w_gate, w_up, w_down):
    tok_rows, model_width = tokens.shape
    top_count = expert_ids.shape[1]
    owners = lax.axis_size("expert")
    capacity = min(tok_rows, 3 * tok_rows * top_count // (2 * owners))
    slot_count = owners * capacity
    flat_ids = expert_ids.reshape(-1)
    pair_count = flat_ids.shape[0]
    picked = (flat_ids[:, None] == jnp.arange(owners, dtype=jnp.int32)[None, :]).astype(jnp.int32)
    before = jnp.cumsum(picked, axis=0) - picked
    position = jnp.sum(before * picked, axis=1)
    target = flat_ids * capacity + position
    source_row = jnp.arange(pair_count, dtype=jnp.int32) // top_count
    send_rows = (
        jnp.zeros((slot_count, model_width), jnp.bfloat16).at[target].set(tokens[source_row])
    )
    send_cot = (
        jnp.zeros((slot_count, model_width), jnp.bfloat16).at[target].set(cotangent[source_row])
    )
    send_gate = jnp.zeros((slot_count,), jnp.bfloat16).at[target].set(gates.reshape(-1))
    recv_gate = lax.all_to_all(
        by_owner(send_gate, owners, capacity), "expert", split_axis=0, concat_axis=0, tiled=True
    )
    recv_rows = lax.all_to_all(
        by_owner(send_rows, owners, capacity), "expert", split_axis=0, concat_axis=0, tiled=True
    )
    recv_cot = lax.all_to_all(
        by_owner(send_cot, owners, capacity), "expert", split_axis=0, concat_axis=0, tiled=True
    )
    rows = recv_rows.reshape(slot_count, model_width)
    cot_rows = recv_cot.reshape(slot_count, model_width)
    gate_column = recv_gate.reshape(slot_count)
    hidden, scaled, grad_pre_gate, grad_pre_up, row_grad, score_grad = expert_pass(
        rows, cot_rows, gate_column, w_gate[0], w_up[0], w_down[0]
    )
    part_gate = contract_rows(rows, grad_pre_gate)
    part_up = contract_rows(rows, grad_pre_up)
    part_down = contract_rows(hidden, scaled)
    back_rows, back_scores = send_back(row_grad, score_grad, owners, capacity)
    summed = sum_weights(part_gate, part_up, part_down)
    pair_rows = back_rows.reshape(slot_count, model_width)[target].reshape(
        tok_rows, top_count, model_width
    )
    grad_tokens = jnp.sum(pair_rows.astype(jnp.float32), axis=1).astype(jnp.bfloat16)
    grad_gates = back_scores.reshape(slot_count)[target].reshape(tok_rows, top_count)
    grad_w_gate = summed[0].astype(jnp.bfloat16)[None]
    grad_w_up = summed[1].astype(jnp.bfloat16)[None]
    grad_w_down = summed[2].astype(jnp.bfloat16)[None]
    return (grad_tokens, grad_gates, grad_w_gate, grad_w_up, grad_w_down)


def slots_of(tok_rows, top_count, owners):
    return min(tok_rows, 3 * tok_rows * top_count // (2 * owners))


def body(tokens, expert_ids, gates, cotangent, w_gate, w_up, w_down):
    capacity = slots_of(tokens.shape[0], expert_ids.shape[1], lax.axis_size("expert"))
    even = lax.axis_size("dp") == 4 and lax.axis_size("expert") == 8
    chosen = kernel_body if even and capacity % 16 == 0 else plain_body
    return chosen(tokens, expert_ids, gates, cotangent, w_gate, w_up, w_down)


def solution(mesh):
    placed = (
        P(("dp", "expert"), None),
        P(("dp", "expert"), None),
        P(("dp", "expert"), None),
        P(("dp", "expert"), None),
        P("expert", None, None),
        P("expert", None, None),
        P("expert", None, None),
    )
    return jax.shard_map(
        body,
        mesh=mesh,
        in_specs=placed,
        out_specs=(
            P(("dp", "expert"), None),
            P(("dp", "expert"), None),
            P("expert", "dp", None),
            P("expert", "dp", None),
            P("expert", None, "dp"),
        ),
        check_vma=False,
    )
```
